512 devices in a mesh: src: 64 (over y, z), tgt: 8 (over x, core).
Axes of the slice: x: 4, y: 8, z: 8, core: 2. Of those that a mesh axis runs over, the one named last changes fastest.
Arguments:
- sources: bfloat16 [16384, 768], P('src'), may hold values from -6 to 6
- targets: bfloat16 [16384, 768], P('tgt'), may hold values from -6 to 6
Outputs:
- barycenters: bfloat16 [16384, 768], P(('src', 'tgt'))
- dual_rows: float32 [16384], P('src')
- dual_cols: float32 [16384], P('tgt')
The draws below stay inside these ranges and needn't reach their ends.
All inputs are finite; a program needn't handle non-finite values.
Results may differ from the reference program's by a relative error of at most 0.004.
Values sent between devices are 32-bit elements; how exact they have to be, the bound alone decides.
A program may use at most 64 MiB of HBM per device.

```python
import math
import jax
import jax.numpy as jnp
from jax import lax

D = 768
ITERS = 3
NS = 16384
NT = 16384


def draw_sources(key, part):
    key = jax.random.fold_in(key, 11)
    key_values = jax.random.fold_in(key, 0)
    values = jnp.clip(jax.random.normal(key_values, (NS, D), jnp.float32), -6.0, 6.0)
    return values.astype(jnp.bfloat16)


def steps_of(own_key, dims, cuts, least, high):
    factor_of = 1.0
    for position, parts in cuts:
        heights = jax.random.uniform(jax.random.fold_in(jax.random.fold_in(own_key, 6), position), (parts,), jnp.float32, least / len(cuts), high / len(cuts))
        factor_of = factor_of * jnp.repeat(jnp.exp(heights), dims[position] // parts).reshape((-1,) + (1,) * (len(dims) - 1 - position))
    return factor_of


def scatter_about(key, shape, scale, limit, cuts=(), held_as=jnp.bfloat16):
    result = scale * jax.random.normal(key, shape, jnp.float32)
    if cuts:
        result = result * steps_of(key, shape, cuts, -0.22, 0.18)
    return jnp.clip(result, -limit, limit).astype(held_as)


def setup_inputs(seed: int = 0) -> dict:
    keys = jax.random.split(jax.random.key(seed), 3)
    return {
        "sources": draw_sources(jax.random.fold_in(keys[2], 71), 0),
        "targets": scatter_about(keys[1], (NT, D), 1.0, 6.0, ((0, 8),)),
    }


entropy = 0.02


def cost_block(src_rows, src_part, targets, tgt_sq):
    cross = jnp.dot(src_rows, targets.T, preferred_element_type=jnp.float32)
    return (src_part[:, None] + tgt_sq[None, :] - 2.0 * cross) / D


def reference(sources, targets):
    block_rows = math.gcd(NS, 512)
    count_blocks = NS // block_rows
    src_sq = jnp.sum(jnp.square(sources.astype(jnp.float32)), axis=1)
    tgt_sq = jnp.sum(jnp.square(targets.astype(jnp.float32)), axis=1)
    src_blocks = sources.reshape(count_blocks, block_rows, D)
    sq_blocks = src_sq.reshape(count_blocks, block_rows)
    log_rows = -math.log(NS)
    log_cols = -math.log(NT)

    def row_update(dual_cols):
        def one_block(pieces):
            rows_here, sq_here = pieces
            scores = (dual_cols[None, :] - cost_block(rows_here, sq_here, targets, tgt_sq)) / entropy
            row_peak = jnp.max(scores, axis=1)
            row_sum = jnp.sum(jnp.exp(scores - row_peak[:, None]), axis=1)
            return entropy * log_rows - entropy * (row_peak + jnp.log(row_sum))
        return lax.map(one_block, (src_blocks, sq_blocks)).reshape(NS)

    def col_update(dual_rows):
        dual_blocks = dual_rows.reshape(count_blocks, block_rows)

        def one_block(carry, pieces):
            run_peak, run_sum = carry
            rows_here, sq_here, dual_here = pieces
            scores = (dual_here[:, None] - cost_block(rows_here, sq_here, targets, tgt_sq)) / entropy
            new_peak = jnp.maximum(run_peak, jnp.max(scores, axis=0))
            new_sum = run_sum * jnp.exp(run_peak - new_peak) + jnp.sum(jnp.exp(scores - new_peak[None, :]), axis=0)
            return (new_peak, new_sum), None

        start = (jnp.full((NT,), -jnp.inf, jnp.float32), jnp.zeros((NT,), jnp.float32))
        (col_peak, col_sum), _ = lax.scan(one_block, start, (src_blocks, sq_blocks, dual_blocks))
        return entropy * log_cols - entropy * (col_peak + jnp.log(col_sum))

    dual_cols = jnp.zeros((NT,), jnp.float32)
    dual_rows = jnp.zeros((NS,), jnp.float32)
    for repeat in range(ITERS):
        dual_rows = row_update(dual_cols)
        dual_cols = col_update(dual_rows)

    def final_block(pieces):
        rows_here, sq_here = pieces
        scores = (dual_cols[None, :] - cost_block(rows_here, sq_here, targets, tgt_sq)) / entropy
        row_peak = jnp.max(scores, axis=1)
        expon = jnp.exp(scores - row_peak[:, None])
        row_sum = jnp.sum(expon, axis=1)
        weights = expon.astype(jnp.bfloat16)
        numer = jnp.dot(weights, targets, preferred_element_type=jnp.float32)
        return (numer / row_sum[:, None]).astype(jnp.bfloat16)

    barycenters = lax.map(final_block, (src_blocks, sq_blocks)).reshape(NS, D)
    return (barycenters, dual_rows, dual_cols)
```

```python
import functools
import math

import jax
import jax.numpy as jnp
from jax import lax
from jax.experimental import pallas as pl
from jax.experimental.pallas import tpu as pltpu
from jax.sharding import PartitionSpec as P

ITERS = 3
ENTROPY = 0.02
SCALE = math.log2(math.e) / ENTROPY
LANES = 128
SUB = 8
MESH = pl.DeviceIdType.MESH


def tree(op, items):
    items = list(items)
    while len(items) > 1:
        paired = [op(items[k], items[k + 1]) for k in range(0, len(items) - 1, 2)]
        if len(items) % 2:
            paired.append(items[-1])
        items = paired
    return items[0]


def lse_of(parts):
    peak = tree(jnp.maximum, parts)
    return peak + jnp.log2(tree(jnp.add, [jnp.exp2(part - peak) for part in parts]))


def lse_down(block):
    peak = jnp.max(block, axis=0, keepdims=True)
    return peak + jnp.log2(jnp.sum(jnp.exp2(block - peak), axis=0, keepdims=True))


def kernel(
    dims, src_ref, tgt_ref, bary_ref, rows_ref, cols_ref,
    scaled, sq_rows, sq_cols, cols_now, across, spread, peaks, weights, numer,
    row_slots, col_first, col_second, numer_slots,
    row_send, row_recv, col_send, col_recv, numer_send, numer_recv,
):
    ys, zs, xs, cores = dims
    tgts = xs * cores
    rows, width = src_ref.shape
    cols = tgt_ref.shape[0]
    row_tiles, col_tiles = rows // LANES, cols // LANES
    half = col_tiles // 2
    share = rows // tgts
    log_rows = math.log2(rows * ys * zs)
    log_cols = math.log2(cols * tgts)
    per_square = SCALE / width

    me_s, me_t = lax.axis_index("src"), lax.axis_index("tgt")
    y, z = lax.div(me_s, zs), lax.rem(me_s, zs)
    x, core = lax.div(me_t, cores), lax.rem(me_t, cores)
    tgt_peers = []
    for dx in range(xs):
        for dc in range(cores):
            if dx or dc:
                tgt_peers.append(lax.rem(x + dx, xs) * cores + lax.rem(core + dc, cores))
    tgt_ids = [(me_s, peer) for peer in tgt_peers]
    y_ids = [(lax.rem(y + d, ys) * zs + z, me_t) for d in range(1, ys)]
    z_ids = [(y * zs + lax.rem(z + d, zs), me_t) for d in range(1, zs)]

    barrier = pltpu.get_barrier_semaphore()
    everyone = tgt_ids + y_ids + z_ids
    for peer in everyone:
        pl.semaphore_signal(barrier, inc=1, device_id=peer, device_id_type=MESH)

    def copy_of(src, dst, send_sem, recv_sem, peer):
        return pltpu.make_async_remote_copy(
            src_ref=src, dst_ref=dst, send_sem=send_sem, recv_sem=recv_sem,
            device_id=peer, device_id_type=MESH,
        )

    def share_slot(slots, me, peers, send_sem, recv_sem):
        for peer in peers:
            copy_of(slots.at[me], slots.at[me], send_sem, recv_sem, peer).start()

    def arrived(slots, peers, send_sem, recv_sem):
        others = slots.at[pl.ds(0, len(peers))]
        copy_of(others, others, send_sem, recv_sem, peers[0]).wait_recv()

    def sent(slots, peers, send_sem, recv_sem):
        others = slots.at[pl.ds(0, len(peers))]
        copy_of(others, others, send_sem, recv_sem, peers[0]).wait_send()

    pair = 2 * LANES

    def product(j, carry):
        start = pl.multiple_of(j * pair, pair)
        block = lax.dot_general(
            src_ref[...], tgt_ref[pl.ds(start, pair), :], (((1,), (1,)), ((), ())),
            preferred_element_type=jnp.float32,
        ) * (2.0 * per_square)
        scaled[2 * j] = block[:, :LANES]
        scaled[2 * j + 1] = block[:, LANES:]
        return carry

    lax.fori_loop(0, cols // pair, product, 0)

    def squares(ref, t):
        start = pl.multiple_of(t * LANES, LANES)
        block = ref[pl.ds(start, LANES), :].astype(jnp.float32)
        block = block * block
        part = tree(jnp.add, [block[:, k * LANES:(k + 1) * LANES] for k in range(width // LANES)])
        return jnp.sum(part.T, axis=0, keepdims=True) * per_square

    def target_squares(t, carry):
        sq_cols[pl.ds(t, 1), :] = squares(tgt_ref, t)
        return carry

    lax.fori_loop(0, col_tiles, target_squares, 0)
    for h in range(row_tiles):
        sq_rows[h:h + 1, :] = squares(src_ref, h)
    cols_now[...] = -sq_cols[...]

    pl.semaphore_wait(barrier, len(everyone))

    def row_lse(step):
        held = [jnp.broadcast_to(cols_now[t:t + 1, :], (SUB, LANES)) for t in range(col_tiles)]

        def body(r, carry):
            at = pl.ds(pl.multiple_of(r * SUB, SUB), SUB)
            across[at, :] = lse_of([scaled[t, at, :] + held[t] for t in range(col_tiles)])
            return carry

        lax.fori_loop(0, rows // SUB, body, 0, unroll=4)
        for h in range(row_tiles):
            row_slots[step, me_t, h:h + 1, :] = lse_down(across[h * LANES:(h + 1) * LANES, :].T)

    def exchange_rows(step):
        share_slot(row_slots.at[step], me_t, tgt_ids, row_send.at[step], row_recv.at[step])

    def rows_total(step):
        arrived(row_slots.at[step], tgt_ids, row_send.at[step], row_recv.at[step])
        return lse_of([row_slots[step, k] for k in range(tgts)])

    def spread_rows(values):
        for h in range(row_tiles):
            block = jnp.broadcast_to(values[h:h + 1, :], (LANES, LANES))
            spread[h * LANES:(h + 1) * LANES, :] = block.T

    def col_lse(step):
        def body(t, carry):
            def term(r):
                return scaled[t, r * SUB:(r + 1) * SUB, :] + spread[r * SUB:(r + 1) * SUB, :]

            peak = tree(jnp.maximum, [term(r) for r in range(rows // SUB)])
            total = tree(jnp.add, [jnp.exp2(term(r) - peak) for r in range(rows // SUB)])
            top = jnp.max(peak, axis=0, keepdims=True)
            summed = jnp.sum(total * jnp.exp2(peak - top), axis=0, keepdims=True)
            cols_now[pl.ds(t, 1), :] = top + jnp.log2(summed)
            return carry

        lax.fori_loop(0, col_tiles, body, 0, unroll=2)
        col_first[step, 0, y] = cols_now[:half, :]
        col_first[step, 1, z] = cols_now[half:, :]

    def exchange_cols(step):
        plan = ((0, y, y_ids), (1, z, z_ids))
        for p, me, peers in plan:
            share_slot(col_first.at[step, p], me, peers, col_send.at[step, 0, p], col_recv.at[step, 0, p])
        turned = ((0, z, z_ids), (1, y, y_ids))
        for (p, me, peers), (_, me_next, peers_next) in zip(plan, turned):
            arrived(col_first.at[step, p], peers, col_send.at[step, 0, p], col_recv.at[step, 0, p])
            col_second[step, p, me_next] = lse_of(
                [col_first[step, p, k] for k in range(len(peers) + 1)]
            )
            share_slot(
                col_second.at[step, p], me_next, peers_next,
                col_send.at[step, 1, p], col_recv.at[step, 1, p],
            )
        for p, me, peers in turned:
            arrived(col_second.at[step, p], peers, col_send.at[step, 1, p], col_recv.at[step, 1, p])
            total = lse_of([col_second[step, p, k] for k in range(len(peers) + 1)])
            cols_now[p * half:(p + 1) * half, :] = -log_cols - total

    for step in range(ITERS):
        row_lse(step)
        exchange_rows(step)
        potential = -log_rows - rows_total(step)
        spread_rows(potential)
        if step == ITERS - 1:
            rows_ref[...] = (potential + sq_rows[...]) * (1.0 / SCALE)
        col_lse(step)
        exchange_cols(step)
    cols_ref[...] = (cols_now[...] + sq_cols[...]) * (1.0 / SCALE)

    def final_rows(r, carry):
        at = pl.ds(pl.multiple_of(r * 2 * SUB, 2 * SUB), 2 * SUB)
        terms = [scaled[t, at, :] + cols_now[t:t + 1, :] for t in range(col_tiles)]
        peak = jnp.max(tree(jnp.maximum, terms), axis=1, keepdims=True)
        values = [jnp.exp2(term - peak) for term in terms]
        for t in range(col_tiles):
            weights[at, t * LANES:(t + 1) * LANES] = values[t].astype(jnp.bfloat16)
        total = jnp.sum(tree(jnp.add, values), axis=1, keepdims=True)
        peaks[at, :] = jnp.broadcast_to(peak, (2 * SUB, LANES))
        across[at, :] = jnp.broadcast_to(peak + jnp.log2(total), (2 * SUB, LANES))
        return carry

    lax.fori_loop(0, rows // (2 * SUB), final_rows, 0, unroll=2)
    for h in range(row_tiles):
        row_slots[ITERS, me_t, h:h + 1, :] = across[h * LANES:(h + 1) * LANES, :].T[0:1, :]
    exchange_rows(ITERS)
    chunk = 2 * LANES
    for n in range(width // chunk):
        numer[:, n * chunk:(n + 1) * chunk] = jnp.dot(
            weights[...], tgt_ref[:, n * chunk:(n + 1) * chunk], preferred_element_type=jnp.float32
        )
    spread_rows(rows_total(ITERS))

    def send_scaled(peer):
        at = pl.ds(pl.multiple_of(peer * share, share), share)
        factor = jnp.exp2(peaks[at, :] - spread[at, :])
        for n in range(width // LANES):
            lanes = slice(n * LANES, (n + 1) * LANES)
            numer[at, lanes] = numer[at, lanes] * factor
        return at

    for peer, ident in zip(tgt_peers, tgt_ids):
        at = send_scaled(peer)
        copy_of(numer.at[at], numer_slots.at[me_t], numer_send, numer_recv, ident).start()
    own = send_scaled(me_t)
    numer_slots[me_t] = numer[own, :]
    arrived(numer_slots, tgt_ids, numer_send, numer_recv)
    bary_ref[...] = tree(jnp.add, [numer_slots[k] for k in range(tgts)]).astype(jnp.bfloat16)

    for step in range(ITERS + 1):
        sent(row_slots.at[step], tgt_ids, row_send.at[step], row_recv.at[step])
    for step in range(ITERS):
        for p, peers, peers_next in ((0, y_ids, z_ids), (1, z_ids, y_ids)):
            sent(col_first.at[step, p], peers, col_send.at[step, 0, p], col_recv.at[step, 0, p])
            sent(col_second.at[step, p], peers_next, col_send.at[step, 1, p], col_recv.at[step, 1, p])
    sent(numer_slots, tgt_ids, numer_send, numer_recv)


def build(mesh, dims):
    ys, zs, xs, cores = dims
    tgts = xs * cores
    most = max(ys, zs)

    def on_device(sources, targets):
        rows, width = sources.shape
        cols = targets.shape[0]
        row_tiles, col_tiles = rows // LANES, cols // LANES
        half, share = col_tiles // 2, rows // tgts
        f32 = jnp.float32
        bary, dual_rows, dual_cols = pl.pallas_call(
            functools.partial(kernel, dims),
            out_shape=(
                jax.ShapeDtypeStruct((share, width), jnp.bfloat16),
                jax.ShapeDtypeStruct((row_tiles, LANES), f32),
                jax.ShapeDtypeStruct((col_tiles, LANES), f32),
            ),
            in_specs=[pl.BlockSpec(memory_space=pltpu.VMEM)] * 2,
            out_specs=[pl.BlockSpec(memory_space=pltpu.VMEM)] * 3,
            scratch_shapes=[
                pltpu.VMEM((col_tiles, rows, LANES), f32),
                pltpu.VMEM((row_tiles, LANES), f32),
                pltpu.VMEM((col_tiles, LANES), f32),
                pltpu.VMEM((col_tiles, LANES), f32),
                pltpu.VMEM((rows, LANES), f32),
                pltpu.VMEM((rows, LANES), f32),
                pltpu.VMEM((rows, LANES), f32),
                pltpu.VMEM((rows, cols), jnp.bfloat16),
                pltpu.VMEM((rows, width), f32),
                pltpu.VMEM((ITERS + 1, tgts, row_tiles, LANES), f32),
                pltpu.VMEM((ITERS, 2, most, half, LANES), f32),
                pltpu.VMEM((ITERS, 2, most, half, LANES), f32),
                pltpu.VMEM((tgts, share, width), f32),
                pltpu.SemaphoreType.DMA((ITERS + 1,)),
                pltpu.SemaphoreType.DMA((ITERS + 1,)),
                pltpu.SemaphoreType.DMA((ITERS, 2, 2)),
                pltpu.SemaphoreType.DMA((ITERS, 2, 2)),
                pltpu.SemaphoreType.DMA,
                pltpu.SemaphoreType.DMA,
            ],
            compiler_params=pltpu.CompilerParams(
                collective_id=0, has_side_effects=True, vmem_limit_bytes=40 * 1024 * 1024
            ),
        )(sources, targets)
        return bary, dual_rows.reshape(rows), dual_cols.reshape(cols)

    in_specs = (P("src", None), P("tgt", None))
    out_specs = (P(("src", "tgt"), None), P("src"), P("tgt"))
    return jax.shard_map(
        on_device, mesh=mesh, in_specs=in_specs, out_specs=out_specs, check_vma=False
    )


def solution(mesh):
    return build(mesh, (8, 8, 4, 2))
```

```python
import functools
import math

import jax
import jax.numpy as jnp
from jax import lax
from jax.experimental import pallas as pl
from jax.experimental.pallas import tpu as pltpu
from jax.sharding import PartitionSpec as P

ITERS = 3
ENTROPY = 0.02
SCALE = math.log2(math.e) / ENTROPY
LANES = 128
SUB = 8
CHUNK = 256
MESH = pl.DeviceIdType.MESH


def tree(op, items):
    items = list(items)
    while len(items) > 1:
        paired = [op(items[k], items[k + 1]) for k in range(0, len(items) - 1, 2)]
        if len(items) % 2:
            paired.append(items[-1])
        items = paired
    return items[0]


def add_up(items):
    return tree(jnp.add, items)


def lse_of(parts):
    peak = tree(jnp.maximum, parts)
    return peak + jnp.log2(add_up([jnp.exp2(part - peak) for part in parts]))


def lse_down(block):
    peak = jnp.max(block, axis=0, keepdims=True)
    return peak + jnp.log2(jnp.sum(jnp.exp2(block - peak), axis=0, keepdims=True))


def farthest_first(n):
    return sorted(range(1, n), key=lambda d: -min(d, n - d))


def kernel(
    dims, src_hbm, tgt_hbm, bary_ref, rows_ref, cols_ref,
    src_ref, tgt_ref, scores, sq_rows, sq_cols, first_rows, first_cols, col_peaks, base, factors,
    across, spread, weights, numer,
    row_slots, col_first, col_second, core_slots, x_slots,
    src_sem, tgt_sem, row_send, row_recv, col_send, col_recv, core_send, core_recv, x_send, x_recv,
):
    ys, zs, xs, cores = dims
    tgts = xs * cores
    rows, width = src_ref.shape
    cols = tgt_ref.shape[0]
    row_tiles, col_tiles = rows // LANES, cols // LANES
    half = col_tiles // 2
    share = rows // tgts
    mine = rows // cores
    log_rows = math.log2(rows * ys * zs)
    log_cols = math.log2(cols * tgts)
    per_square = SCALE / width

    me_s, me_t = lax.axis_index("src"), lax.axis_index("tgt")
    y, z = lax.div(me_s, zs), lax.rem(me_s, zs)
    x, core = lax.div(me_t, cores), lax.rem(me_t, cores)
    other = 1 - core

    def tgt_id(dx, which):
        return (me_s, lax.rem(x + dx, xs) * cores + which)

    x_order = farthest_first(xs)
    tgt_ids = [tgt_id(dx, which) for dx in x_order for which in (other, core)] + [tgt_id(0, other)]
    y_ids = [(lax.rem(y + d, ys) * zs + z, me_t) for d in farthest_first(ys)]
    z_ids = [(y * zs + lax.rem(z + d, zs), me_t) for d in farthest_first(zs)]

    barrier = pltpu.get_barrier_semaphore()
    everyone = y_ids + z_ids + tgt_ids
    for peer in everyone:
        pl.semaphore_signal(barrier, inc=1, device_id=peer, device_id_type=MESH)

    src_copy = pltpu.make_async_copy(src_hbm, src_ref, src_sem)
    src_copy.start()
    tgt_copies = []
    for j in range(cols // CHUNK):
        at = pl.ds(j * CHUNK, CHUNK)
        tgt_copies.append(pltpu.make_async_copy(tgt_hbm.at[at], tgt_ref.at[at], tgt_sem.at[j]))
        tgt_copies[-1].start()

    def copy_of(src, dst, send_sem, recv_sem, peer):
        return pltpu.make_async_remote_copy(
            src_ref=src, dst_ref=dst, send_sem=send_sem, recv_sem=recv_sem,
            device_id=peer, device_id_type=MESH,
        )

    def share_slot(slots, me, peers, send_sem, recv_sem):
        for peer in peers:
            copy_of(slots.at[me], slots.at[me], send_sem, recv_sem, peer).start()

    def arrived(slots, peers, send_sem, recv_sem):
        others = slots.at[pl.ds(0, len(peers))]
        copy_of(others, others, send_sem, recv_sem, peers[0]).wait_recv()

    def sent(slots, peers, send_sem, recv_sem):
        others = slots.at[pl.ds(0, len(peers))]
        copy_of(others, others, send_sem, recv_sem, peers[0]).wait_send()

    def squares(ref, t):
        block = ref[t * LANES:(t + 1) * LANES, :].astype(jnp.float32)
        block = block * block
        part = add_up([block[:, k * LANES:(k + 1) * LANES] for k in range(width // LANES)])
        return jnp.sum(part.T, axis=0, keepdims=True) * per_square

    src_copy.wait()
    for h in range(row_tiles):
        sq_rows[h:h + 1, :] = squares(src_ref, h)
    for j in range(cols // CHUNK):
        tgt_copies[j].wait()
        block = lax.dot_general(
            src_ref[...], tgt_ref[j * CHUNK:(j + 1) * CHUNK, :], (((1,), (1,)), ((), ())),
            preferred_element_type=jnp.float32,
        ) * (2.0 * per_square)
        for k in range(CHUNK // LANES):
            t = j * (CHUNK // LANES) + k
            scores[t] = block[:, k * LANES:(k + 1) * LANES]
            sq_cols[t:t + 1, :] = squares(tgt_ref, t)

    held = [jnp.broadcast_to(sq_cols[t:t + 1, :], (SUB, LANES)) for t in range(col_tiles)]

    def first_row_body(r, carry):
        at = pl.ds(pl.multiple_of(r * SUB, SUB), SUB)
        across[at, :] = lse_of([scores[t, at, :] - held[t] for t in range(col_tiles)])
        return carry

    lax.fori_loop(0, rows // SUB, first_row_body, 0, unroll=8)
    for h in range(row_tiles):
        row_slots[0, me_t, h:h + 1, :] = lse_down(across[h * LANES:(h + 1) * LANES, :].T)

    pl.semaphore_wait(barrier, len(everyone))

    def send_rows(step):
        share_slot(row_slots.at[step], me_t, tgt_ids, row_send.at[step], row_recv.at[step])

    def rows_here(step):
        arrived(row_slots.at[step], tgt_ids, row_send.at[step], row_recv.at[step])
        return [row_slots[step, k] for k in range(tgts)]

    def spread_rows(values):
        for h in range(row_tiles):
            block = jnp.broadcast_to(values[h:h + 1, :], (LANES, LANES))
            spread[h * LANES:(h + 1) * LANES, :] = block.T

    first_leg = ((y, y_ids), (z, z_ids))
    second_leg = ((z, z_ids), (y, y_ids))

    def send_cols(step, p):
        me, peers = first_leg[p]
        share_slot(col_first.at[step, p], me, peers, col_send.at[step, 0, p], col_recv.at[step, 0, p])

    def turn_cols(step, p, combine):
        peers = first_leg[p][1]
        arrived(col_first.at[step, p], peers, col_send.at[step, 0, p], col_recv.at[step, 0, p])
        me, peers_next = second_leg[p]
        col_second[step, p, me] = combine([col_first[step, p, k] for k in range(len(peers) + 1)])
        share_slot(
            col_second.at[step, p], me, peers_next, col_send.at[step, 1, p], col_recv.at[step, 1, p]
        )

    def cols_here(step, p, combine):
        peers = second_leg[p][1]
        arrived(col_second.at[step, p], peers, col_send.at[step, 1, p], col_recv.at[step, 1, p])
        return combine([col_second[step, p, k] for k in range(len(peers) + 1)])

    def first_col_body(p):
        me = first_leg[p][0]

        def body(k, carry):
            t = p * half + k

            def term(r):
                return scores[t, r * SUB:(r + 1) * SUB, :] + spread[r * SUB:(r + 1) * SUB, :]

            peak = tree(jnp.maximum, [term(r) for r in range(rows // SUB)])
            peak = jnp.max(peak, axis=0, keepdims=True)
            sums = []
            for r in range(rows // SUB):
                value = jnp.exp2(term(r) - peak)
                scores[t, r * SUB:(r + 1) * SUB, :] = value
                sums.append(value)
            total = jnp.sum(add_up(sums), axis=0, keepdims=True)
            col_peaks[pl.ds(t, 1), :] = peak
            col_first[0, p, me, pl.ds(k, 1), :] = peak + jnp.log2(total)
            return carry

        return body

    def col_body(step, p):
        me = first_leg[p][0]

        def body(k, carry):
            t = p * half + k
            total = add_up(
                [scores[t, r * SUB:(r + 1) * SUB, :] * spread[r * SUB:(r + 1) * SUB, :]
                 for r in range(rows // SUB)]
            )
            total = jnp.sum(total, axis=0, keepdims=True) * base[pl.ds(t, 1), :]
            col_first[step, p, me, pl.ds(k, 1), :] = total
            return carry

        return body

    for step in range(ITERS):
        send_rows(step)
        if step == 0:
            potential = -log_rows - lse_of(rows_here(step))
            first_rows[...] = potential
            spread_rows(potential)
        else:
            scale = 1.0 / (add_up(rows_here(step)) * (2.0 ** log_rows))
            spread_rows(scale)
            if step == ITERS - 1:
                final = first_rows[...] + jnp.log2(scale) + sq_rows[...]
                rows_ref[...] = final * (1.0 / SCALE)
        for p in range(2):
            body = col_body(step, p) if step else first_col_body(p)
            lax.fori_loop(0, half, body, 0, unroll=4)
            send_cols(step, p)
        combine = add_up if step else lse_of
        for p in range(2):
            turn_cols(step, p, combine)
        for p in range(2):
            at = slice(p * half, (p + 1) * half)
            total = cols_here(step, p, combine)
            if step == 0:
                potential = -log_cols - total
                first_cols[at, :] = potential
                base[at, :] = jnp.exp2(col_peaks[at, :] + potential)
                factors[at, :] = base[at, :]
            else:
                scale = 1.0 / (total * (2.0 ** log_cols))
                factors[at, :] = base[at, :] * scale
                if step == ITERS - 1:
                    final = first_cols[at, :] + jnp.log2(scale) + sq_cols[at, :]
                    cols_ref[at, :] = final * (1.0 / SCALE)
            if step < ITERS - 1:
                held = [
                    jnp.broadcast_to(factors[p * half + k:p * half + k + 1, :], (SUB, LANES))
                    for k in range(half)
                ]

                def row_body(r, carry, p=p, held=held):
                    at = pl.ds(pl.multiple_of(r * SUB, SUB), SUB)
                    terms = [scores[p * half + k, at, :] * held[k] for k in range(half)]
                    if p:
                        terms.append(across[at, :])
                    across[at, :] = add_up(terms)
                    return carry

                lax.fori_loop(0, rows // SUB, row_body, 0, unroll=8)
        if step < ITERS - 1:
            for h in range(row_tiles):
                total = jnp.sum(across[h * LANES:(h + 1) * LANES, :].T, axis=0, keepdims=True)
                row_slots[step + 1, me_t, h:h + 1, :] = total

    tall = 2 * SUB

    def weight_body(b, carry):
        place = lax.div(b * tall, share)
        within = lax.rem(b * tall, share)
        which = lax.rem(other + lax.div(place, xs), cores)
        start = (lax.rem(place, xs) * cores + which) * share + within
        at = pl.ds(pl.multiple_of(start, tall), tall)
        to = pl.ds(pl.multiple_of(b * tall, tall), tall)
        values = [scores[t, at, :] * factors[t:t + 1, :] for t in range(col_tiles)]
        for t in range(col_tiles):
            weights[to, t * LANES:(t + 1) * LANES] = values[t].astype(jnp.bfloat16)
        across[at, :] = add_up(values)
        return carry

    lax.fori_loop(0, rows // tall, weight_body, 0, unroll=4)
    chunks = width // CHUNK
    sibling = tgt_id(0, other)

    def core_copy(n):
        return copy_of(
            numer.at[n, pl.ds(0, mine)], core_slots.at[n], core_send.at[n], core_recv.at[n], sibling
        )

    for n in range(chunks):
        numer[n] = jnp.dot(
            weights[...], tgt_ref[:, n * CHUNK:(n + 1) * CHUNK], preferred_element_type=jnp.float32
        )
        core_copy(n).start()
    for h in range(row_tiles):
        total = jnp.sum(across[h * LANES:(h + 1) * LANES, :].T, axis=0, keepdims=True)
        row_slots[ITERS, me_t, h:h + 1, :] = total
    send_rows(ITERS)

    def x_part(n, dx):
        place = lax.rem(x + dx, xs) * share
        return (
            pl.ds(pl.multiple_of(mine + place, share), share),
            pl.ds(pl.multiple_of(place, share), share),
        )

    for n in range(chunks):
        core_copy(n).wait_recv()
        for k, dx in enumerate(x_order):
            own, got = x_part(n, dx)
            numer[n, own, :] = numer[n, own, :] + core_slots[n, got, :]
            copy_of(
                numer.at[n, own], x_slots.at[n, k], x_send.at[n], x_recv.at[n], tgt_id(dx, core)
            ).start()

    spread_rows(1.0 / add_up(rows_here(ITERS)))
    scale = spread[pl.ds(pl.multiple_of(me_t * share, share), share), :]

    def x_wait(n):
        return copy_of(x_slots.at[n], x_slots.at[n], x_send.at[n], x_recv.at[n], sibling)

    for n in range(chunks):
        own, got = x_part(n, 0)
        near = numer[n, own, :] + core_slots[n, got, :]
        x_wait(n).wait_recv()
        total = near + add_up([x_slots[n, k] for k in range(xs - 1)])
        for k in range(CHUNK // LANES):
            piece = total[:, k * LANES:(k + 1) * LANES] * scale
            start = n * CHUNK + k * LANES
            bary_ref[:, start:start + LANES] = piece.astype(jnp.bfloat16)

    for step in range(ITERS + 1):
        sent(row_slots.at[step], tgt_ids, row_send.at[step], row_recv.at[step])
    for step in range(ITERS):
        for p in range(2):
            for leg, slots, plan in ((0, col_first, first_leg), (1, col_second, second_leg)):
                sent(
                    slots.at[step, p], plan[p][1], col_send.at[step, leg, p], col_recv.at[step, leg, p]
                )
    for n in range(chunks):
        core_copy(n).wait_send()
        x_wait(n).wait_send()


def build(mesh, dims):
    ys, zs, xs, cores = dims
    tgts = xs * cores
    most = max(ys, zs)

    def on_device(sources, targets):
        rows, width = sources.shape
        cols = targets.shape[0]
        row_tiles, col_tiles = rows // LANES, cols // LANES
        half, share, chunks = col_tiles // 2, rows // tgts, width // CHUNK
        f32 = jnp.float32
        dma = pltpu.SemaphoreType.DMA
        bary, dual_rows, dual_cols = pl.pallas_call(
            functools.partial(kernel, dims),
            out_shape=(
                jax.ShapeDtypeStruct((share, width), jnp.bfloat16),
                jax.ShapeDtypeStruct((row_tiles, LANES), f32),
                jax.ShapeDtypeStruct((col_tiles, LANES), f32),
            ),
            in_specs=[pl.BlockSpec(memory_space=pl.ANY)] * 2,
            out_specs=[pl.BlockSpec(memory_space=pltpu.VMEM)] * 3,
            scratch_shapes=[
                pltpu.VMEM((rows, width), jnp.bfloat16),
                pltpu.VMEM((cols, width), jnp.bfloat16),
                pltpu.VMEM((col_tiles, rows, LANES), f32),
                pltpu.VMEM((row_tiles, LANES), f32),
                pltpu.VMEM((col_tiles, LANES), f32),
                pltpu.VMEM((row_tiles, LANES), f32),
                pltpu.VMEM((col_tiles, LANES), f32),
                pltpu.VMEM((col_tiles, LANES), f32),
                pltpu.VMEM((col_tiles, LANES), f32),
                pltpu.VMEM((col_tiles, LANES), f32),
                pltpu.VMEM((rows, LANES), f32),
                pltpu.VMEM((rows, LANES), f32),
                pltpu.VMEM((rows, cols), jnp.bfloat16),
                pltpu.VMEM((chunks, rows, CHUNK), f32),
                pltpu.VMEM((ITERS + 1, tgts, row_tiles, LANES), f32),
                pltpu.VMEM((ITERS, 2, most, half, LANES), f32),
                pltpu.VMEM((ITERS, 2, most, half, LANES), f32),
                pltpu.VMEM((chunks, rows // cores, CHUNK), f32),
                pltpu.VMEM((chunks, xs - 1, share, CHUNK), f32),
                dma,
                dma((cols // CHUNK,)),
                dma((ITERS + 1,)),
                dma((ITERS + 1,)),
                dma((ITERS, 2, 2)),
                dma((ITERS, 2, 2)),
                dma((chunks,)),
                dma((chunks,)),
                dma((chunks,)),
                dma((chunks,)),
            ],
            compiler_params=pltpu.CompilerParams(
                collective_id=0, has_side_effects=True, vmem_limit_bytes=56 * 1024 * 1024
            ),
        )(sources, targets)
        return bary, dual_rows.reshape(rows), dual_cols.reshape(cols)

    in_specs = (P("src", None), P("tgt", None))
    out_specs = (P(("src", "tgt"), None), P("src"), P("tgt"))
    return jax.shard_map(
        on_device, mesh=mesh, in_specs=in_specs, out_specs=out_specs, check_vma=False
    )


def solution(mesh):
    return build(mesh, (8, 8, 4, 2))
```

```python
import functools
import math

import jax
import jax.numpy as jnp
from jax import lax
from jax.experimental import pallas as pl
from jax.experimental.pallas import tpu as pltpu
from jax.sharding import PartitionSpec as P

ITERS = 3
ENTROPY = 0.02
SCALE = math.log2(math.e) / ENTROPY
LANES = 128
SUB = 8
CHUNK = 256
LOAD = 1024
VMEM_GRANT = 55040 * 1024
MESH = pl.DeviceIdType.MESH


def tree(op, items):
    items = list(items)
    while len(items) > 1:
        paired = [op(items[k], items[k + 1]) for k in range(0, len(items) - 1, 2)]
        if len(items) % 2:
            paired.append(items[-1])
        items = paired
    return items[0]


def add_up(items):
    return tree(jnp.add, items)


def lse_of(parts):
    peak = tree(jnp.maximum, parts)
    return peak + jnp.log2(add_up([jnp.exp2(part - peak) for part in parts]))


def lse_down(block):
    peak = jnp.max(block, axis=0, keepdims=True)
    return peak + jnp.log2(jnp.sum(jnp.exp2(block - peak), axis=0, keepdims=True))


def farthest_first(n):
    return sorted(range(1, n), key=lambda d: -min(d, n - d))


def kernel(
    dims, src_hbm, tgt_hbm, bary_ref, rows_ref, cols_ref,
    src_ref, tgt_ref, scores, sq_rows, sq_cols, first_rows, first_cols, col_peaks, base, factors, col_scale,
    across, spread, weights, numer,
    row_slots, col_first, col_second, core_slots, x_slots,
    src_sem, tgt_sem, row_send, row_recv, col_send, col_recv, core_send, core_recv, x_send, x_recv,
):
    ys, zs, xs, cores = dims
    tgts = xs * cores
    rows, width = src_ref.shape
    cols = tgt_ref.shape[0]
    row_tiles, col_tiles = rows // LANES, cols // LANES
    half = col_tiles // 2
    share = rows // tgts
    mine = rows // cores
    log_rows = math.log2(rows * ys * zs)
    log_cols = math.log2(cols * tgts)
    per_square = SCALE / width

    me_s, me_t = lax.axis_index("src"), lax.axis_index("tgt")
    y, z = lax.div(me_s, zs), lax.rem(me_s, zs)
    x, core = lax.div(me_t, cores), lax.rem(me_t, cores)
    other = 1 - core

    def tgt_id(dx, which):
        return (me_s, lax.rem(x + dx, xs) * cores + which)

    x_order = farthest_first(xs)
    tgt_ids = [tgt_id(dx, which) for dx in x_order for which in (other, core)] + [tgt_id(0, other)]
    y_ids = [(lax.rem(y + d, ys) * zs + z, me_t) for d in farthest_first(ys)]
    z_ids = [(y * zs + lax.rem(z + d, zs), me_t) for d in farthest_first(zs)]

    src_copy = pltpu.make_async_copy(src_hbm, src_ref, src_sem)
    src_copy.start()
    tgt_copies = []
    for j in range(cols // LOAD):
        at = pl.ds(j * LOAD, LOAD)
        tgt_copies.append(pltpu.make_async_copy(tgt_hbm.at[at], tgt_ref.at[at], tgt_sem.at[j]))
        tgt_copies[-1].start()

    barrier = pltpu.get_barrier_semaphore()
    everyone = y_ids + z_ids + tgt_ids
    for peer in everyone:
        pl.semaphore_signal(barrier, inc=1, device_id=peer, device_id_type=MESH)

    def copy_of(src, dst, send_sem, recv_sem, peer):
        return pltpu.make_async_remote_copy(
            src_ref=src, dst_ref=dst, send_sem=send_sem, recv_sem=recv_sem,
            device_id=peer, device_id_type=MESH,
        )

    def share_slot(slots, me, peers, send_sem, recv_sem):
        for peer in peers:
            copy_of(slots.at[me], slots.at[me], send_sem, recv_sem, peer).start()

    def share_both(slots, legs, send_sem, recv_sem):
        longest = max(len(peers) for _, peers in legs)
        for k in range(longest):
            for p, (me, peers) in enumerate(legs):
                if k < len(peers):
                    slot = slots.at[p, me]
                    copy_of(slot, slot, send_sem.at[p], recv_sem.at[p], peers[k]).start()

    def arrived(slots, peers, send_sem, recv_sem):
        others = slots.at[pl.ds(0, len(peers))]
        copy_of(others, others, send_sem, recv_sem, peers[0]).wait_recv()

    def sent(slots, peers, send_sem, recv_sem):
        others = slots.at[pl.ds(0, len(peers))]
        copy_of(others, others, send_sem, recv_sem, peers[0]).wait_send()

    def squares(ref, t):
        block = ref[t * LANES:(t + 1) * LANES, :].astype(jnp.float32)
        block = block * block
        part = add_up([block[:, k * LANES:(k + 1) * LANES] for k in range(width // LANES)])
        return jnp.sum(part.T, axis=0, keepdims=True) * per_square

    src_copy.wait()
    for j in range(cols // LOAD):
        tgt_copies[j].wait()
        for i in range(LOAD // CHUNK):
            start = j * LOAD + i * CHUNK
            block = lax.dot_general(
                src_ref[...], tgt_ref[start:start + CHUNK, :], (((1,), (1,)), ((), ())),
                preferred_element_type=jnp.float32,
            ) * (2.0 * per_square)
            for k in range(CHUNK // LANES):
                scores[start // LANES + k] = block[:, k * LANES:(k + 1) * LANES]
        for k in range(LOAD // LANES):
            t = j * (LOAD // LANES) + k
            sq_cols[t:t + 1, :] = squares(tgt_ref, t)

    held = [jnp.broadcast_to(sq_cols[t:t + 1, :], (SUB, LANES)) for t in range(col_tiles)]

    def first_row_body(r, carry):
        at = pl.ds(pl.multiple_of(r * SUB, SUB), SUB)
        across[at, :] = lse_of([scores[t, at, :] - held[t] for t in range(col_tiles)])
        return carry

    lax.fori_loop(0, rows // SUB, first_row_body, 0, unroll=8)
    for h in range(row_tiles):
        row_slots[0, me_t, h:h + 1, :] = lse_down(across[h * LANES:(h + 1) * LANES, :].T)

    pl.semaphore_wait(barrier, len(everyone))

    def send_rows(step):
        share_slot(row_slots.at[step], me_t, tgt_ids, row_send.at[step], row_recv.at[step])

    def rows_here(step):
        arrived(row_slots.at[step], tgt_ids, row_send.at[step], row_recv.at[step])
        return [row_slots[step, k] for k in range(tgts)]

    def spread_rows(values):
        for h in range(row_tiles):
            block = jnp.broadcast_to(values[h:h + 1, :], (LANES, LANES))
            spread[h * LANES:(h + 1) * LANES, :] = block.T

    first_leg = ((y, y_ids), (z, z_ids))
    second_leg = ((z, z_ids), (y, y_ids))

    def send_cols(step):
        share_both(col_first.at[step], first_leg, col_send.at[step, 0], col_recv.at[step, 0])

    def turn_cols(step, combine):
        for p in range(2):
            peers = first_leg[p][1]
            arrived(col_first.at[step, p], peers, col_send.at[step, 0, p], col_recv.at[step, 0, p])
            col_second[step, p, second_leg[p][0]] = combine(
                [col_first[step, p, k] for k in range(len(peers) + 1)]
            )
        share_both(col_second.at[step], second_leg, col_send.at[step, 1], col_recv.at[step, 1])

    def cols_here(step, p, combine):
        peers = second_leg[p][1]
        arrived(col_second.at[step, p], peers, col_send.at[step, 1, p], col_recv.at[step, 1, p])
        return combine([col_second[step, p, k] for k in range(len(peers) + 1)])

    def first_col_body(p):
        me = first_leg[p][0]

        def body(k, carry):
            t = p * half + k

            def term(r):
                return scores[t, r * SUB:(r + 1) * SUB, :] + spread[r * SUB:(r + 1) * SUB, :]

            peak = tree(jnp.maximum, [term(r) for r in range(rows // SUB)])
            peak = jnp.max(peak, axis=0, keepdims=True)
            sums = []
            for r in range(rows // SUB):
                value = jnp.exp2(term(r) - peak)
                scores[t, r * SUB:(r + 1) * SUB, :] = value
                sums.append(value)
            total = jnp.sum(add_up(sums), axis=0, keepdims=True)
            col_peaks[pl.ds(t, 1), :] = peak
            col_first[0, p, me, pl.ds(k, 1), :] = peak + jnp.log2(total)
            return carry

        return body

    def col_body(step, p):
        me = first_leg[p][0]

        def body(k, carry):
            t = p * half + k
            total = add_up(
                [scores[t, r * SUB:(r + 1) * SUB, :] * spread[r * SUB:(r + 1) * SUB, :]
                 for r in range(rows // SUB)]
            )
            total = jnp.sum(total, axis=0, keepdims=True) * base[pl.ds(t, 1), :]
            col_first[step, p, me, pl.ds(k, 1), :] = total
            return carry

        return body

    for step in range(ITERS):
        send_rows(step)
        if step == 0:
            potential = -log_rows - lse_of(rows_here(step))
            first_rows[...] = potential
            spread_rows(potential)
        else:
            scale = 1.0 / (add_up(rows_here(step)) * (2.0 ** log_rows))
            spread_rows(scale)
        for p in range(2):
            body = col_body(step, p) if step else first_col_body(p)
            lax.fori_loop(0, half, body, 0, unroll=8 if step else 4)
        send_cols(step)
        if step == 0:
            for h in range(row_tiles):
                sq_rows[h:h + 1, :] = squares(src_ref, h)
        if step == ITERS - 1:
            final = first_rows[...] + (jnp.log2(scale) if step else 0.0) + sq_rows[...]
            rows_ref[...] = final * (1.0 / SCALE)
        combine = add_up if step else lse_of
        turn_cols(step, combine)
        for p in range(2):
            at = slice(p * half, (p + 1) * half)
            total = cols_here(step, p, combine)
            if step == 0:
                potential = -log_cols - total
                first_cols[at, :] = potential
                base[at, :] = jnp.exp2(col_peaks[at, :] + potential)
                factors[at, :] = base[at, :]
            else:
                scale = 1.0 / (total * (2.0 ** log_cols))
                factors[at, :] = base[at, :] * scale
                col_scale[at, :] = scale
            if step < ITERS - 1:
                held = [
                    jnp.broadcast_to(factors[p * half + k:p * half + k + 1, :], (SUB, LANES))
                    for k in range(half)
                ]

                def row_body(r, carry, p=p, held=held):
                    at = pl.ds(pl.multiple_of(r * SUB, SUB), SUB)
                    terms = [scores[p * half + k, at, :] * held[k] for k in range(half)]
                    if p:
                        terms.append(across[at, :])
                    across[at, :] = add_up(terms)
                    return carry

                lax.fori_loop(0, rows // SUB, row_body, 0, unroll=8)
        if step < ITERS - 1:
            for h in range(row_tiles):
                total = jnp.sum(across[h * LANES:(h + 1) * LANES, :].T, axis=0, keepdims=True)
                row_slots[step + 1, me_t, h:h + 1, :] = total

    tall = 2 * SUB

    def weight_body(b, carry):
        place = lax.div(b * tall, share)
        within = lax.rem(b * tall, share)
        which = lax.rem(other + lax.div(place, xs), cores)
        start = (lax.rem(place, xs) * cores + which) * share + within
        at = pl.ds(pl.multiple_of(start, tall), tall)
        to = pl.ds(pl.multiple_of(b * tall, tall), tall)
        values = [scores[t, at, :] * factors[t:t + 1, :] for t in range(col_tiles)]
        for t in range(col_tiles):
            weights[to, t * LANES:(t + 1) * LANES] = values[t].astype(jnp.bfloat16)
        across[at, :] = add_up(values)
        return carry

    lax.fori_loop(0, rows // tall, weight_body, 0, unroll=4)
    chunks = width // CHUNK
    sibling = tgt_id(0, other)

    def core_copy(n):
        return copy_of(
            numer.at[n, pl.ds(0, mine)], core_slots.at[n], core_send.at[n], core_recv.at[n], sibling
        )

    for n in range(chunks):
        numer[n] = jnp.dot(
            weights[...], tgt_ref[:, n * CHUNK:(n + 1) * CHUNK], preferred_element_type=jnp.float32
        )
        core_copy(n).start()
    for h in range(row_tiles):
        total = jnp.sum(across[h * LANES:(h + 1) * LANES, :].T, axis=0, keepdims=True)
        row_slots[ITERS, me_t, h:h + 1, :] = total
    send_rows(ITERS)

    def x_part(n, dx):
        place = lax.rem(x + dx, xs) * share
        return (
            pl.ds(pl.multiple_of(mine + place, share), share),
            pl.ds(pl.multiple_of(place, share), share),
        )

    for n in range(chunks):
        core_copy(n).wait_recv()
        for k, dx in enumerate(x_order):
            own, got = x_part(n, dx)
            numer[n, own, :] = numer[n, own, :] + core_slots[n, got, :]
            copy_of(
                numer.at[n, own], x_slots.at[n, k], x_send.at[n], x_recv.at[n], tgt_id(dx, core)
            ).start()

    final = first_cols[...] + jnp.log2(col_scale[...]) + sq_cols[...]
    cols_ref[...] = final * (1.0 / SCALE)
    spread_rows(1.0 / add_up(rows_here(ITERS)))
    scale = spread[pl.ds(pl.multiple_of(me_t * share, share), share), :]

    def x_wait(n):
        return copy_of(x_slots.at[n], x_slots.at[n], x_send.at[n], x_recv.at[n], sibling)

    for n in range(chunks):
        own, got = x_part(n, 0)
        near = numer[n, own, :] + core_slots[n, got, :]
        x_wait(n).wait_recv()
        total = near + add_up([x_slots[n, k] for k in range(xs - 1)])
        for k in range(CHUNK // LANES):
            piece = total[:, k * LANES:(k + 1) * LANES] * scale
            start = n * CHUNK + k * LANES
            bary_ref[:, start:start + LANES] = piece.astype(jnp.bfloat16)

    for step in range(ITERS + 1):
        sent(row_slots.at[step], tgt_ids, row_send.at[step], row_recv.at[step])
    for step in range(ITERS):
        for p in range(2):
            for leg, slots, plan in ((0, col_first, first_leg), (1, col_second, second_leg)):
                sent(
                    slots.at[step, p], plan[p][1], col_send.at[step, leg, p], col_recv.at[step, leg, p]
                )
    for n in range(chunks):
        core_copy(n).wait_send()
        x_wait(n).wait_send()


def emit(bary, rows, cols, bary_out, rows_out, cols_out, sems):
    copies = [
        pltpu.make_async_copy(held, out, sems.at[k])
        for k, (held, out) in enumerate(((bary, bary_out), (rows, rows_out), (cols, cols_out)))
    ]
    for copy in copies:
        copy.start()
    for copy in copies:
        copy.wait()


def build(mesh, dims):
    ys, zs, xs, cores = dims
    tgts = xs * cores
    most = max(ys, zs)

    def on_device(sources, targets):
        rows, width = sources.shape
        cols = targets.shape[0]
        row_tiles, col_tiles = rows // LANES, cols // LANES
        half, share, chunks = col_tiles // 2, rows // tgts, width // CHUNK
        f32 = jnp.float32
        dma = pltpu.SemaphoreType.DMA
        bary, dual_rows, dual_cols = pl.pallas_call(
            functools.partial(kernel, dims),
            out_shape=(
                jax.ShapeDtypeStruct((share, width), jnp.bfloat16),
                jax.ShapeDtypeStruct((row_tiles, LANES), f32),
                jax.ShapeDtypeStruct((col_tiles, LANES), f32),
            ),
            in_specs=[pl.BlockSpec(memory_space=pl.ANY)] * 2,
            out_specs=[pl.BlockSpec(memory_space=pltpu.VMEM)] * 3,
            scratch_shapes=[
                pltpu.VMEM((rows, width), jnp.bfloat16),
                pltpu.VMEM((cols, width), jnp.bfloat16),
                pltpu.VMEM((col_tiles, rows, LANES), f32),
                pltpu.VMEM((row_tiles, LANES), f32),
                pltpu.VMEM((col_tiles, LANES), f32),
                pltpu.VMEM((row_tiles, LANES), f32),
                pltpu.VMEM((col_tiles, LANES), f32),
                pltpu.VMEM((col_tiles, LANES), f32),
                pltpu.VMEM((col_tiles, LANES), f32),
                pltpu.VMEM((col_tiles, LANES), f32),
                pltpu.VMEM((col_tiles, LANES), f32),
                pltpu.VMEM((rows, LANES), f32),
                pltpu.VMEM((rows, LANES), f32),
                pltpu.VMEM((rows, cols), jnp.bfloat16),
                pltpu.VMEM((chunks, rows, CHUNK), f32),
                pltpu.VMEM((ITERS + 1, tgts, row_tiles, LANES), f32),
                pltpu.VMEM((ITERS, 2, most, half, LANES), f32),
                pltpu.VMEM((ITERS, 2, most, half, LANES), f32),
                pltpu.VMEM((chunks, rows // cores, CHUNK), f32),
                pltpu.VMEM((chunks, xs - 1, share, CHUNK), f32),
                dma,
                dma((cols // LOAD,)),
                dma((ITERS + 1,)),
                dma((ITERS + 1,)),
                dma((ITERS, 2, 2)),
                dma((ITERS, 2, 2)),
                dma((chunks,)),
                dma((chunks,)),
                dma((chunks,)),
                dma((chunks,)),
            ],
            compiler_params=pltpu.CompilerParams(
                collective_id=0, has_side_effects=True, vmem_limit_bytes=VMEM_GRANT
            ),
        )(sources, targets)
        bary, dual_rows, dual_cols = pl.pallas_call(
            emit,
            out_shape=(
                jax.ShapeDtypeStruct(bary.shape, bary.dtype),
                jax.ShapeDtypeStruct(dual_rows.shape, f32),
                jax.ShapeDtypeStruct(dual_cols.shape, f32),
            ),
            in_specs=[pl.BlockSpec(memory_space=pl.ANY)] * 3,
            out_specs=[pl.BlockSpec(memory_space=pl.ANY)] * 3,
            scratch_shapes=[dma((3,))],
            compiler_params=pltpu.CompilerParams(vmem_limit_bytes=1024 * 1024),
        )(bary, dual_rows, dual_cols)
        return bary, dual_rows.reshape(rows), dual_cols.reshape(cols)

    in_specs = (P("src", None), P("tgt", None))
    out_specs = (P(("src", "tgt"), None), P("src"), P("tgt"))
    return jax.shard_map(
        on_device, mesh=mesh, in_specs=in_specs, out_specs=out_specs, check_vma=False
    )


def solution(mesh):
    return build(mesh, (8, 8, 4, 2))
```

```python
import functools
import math

import jax
import jax.numpy as jnp
from jax import lax
from jax.experimental import pallas as pl
from jax.experimental.pallas import tpu as pltpu
from jax.sharding import PartitionSpec as P

ITERS = 3
ENTROPY = 0.02
SCALE = math.log2(math.e) / ENTROPY
LANES = 128
SUB = 8
CHUNK = 256
LOAD = 1024
VMEM_GRANT = 55040 * 1024
MESH = pl.DeviceIdType.MESH


def tree(op, items):
    items = list(items)
    while len(items) > 1:
        paired = [op(items[k], items[k + 1]) for k in range(0, len(items) - 1, 2)]
        if len(items) % 2:
            paired.append(items[-1])
        items = paired
    return items[0]


def add_up(items):
    return tree(jnp.add, items)


def lse_of(parts):
    peak = tree(jnp.maximum, parts)
    return peak + jnp.log2(add_up([jnp.exp2(part - peak) for part in parts]))


def lse_down(block):
    peak = jnp.max(block, axis=0, keepdims=True)
    return peak + jnp.log2(jnp.sum(jnp.exp2(block - peak), axis=0, keepdims=True))


def farthest_first(n):
    return sorted(range(1, n), key=lambda d: -min(d, n - d))


def kernel(
    dims, src_hbm, tgt_hbm, bary_ref, rows_ref, cols_ref,
    src_ref, tgt_ref, scores, sq_rows, sq_cols, first_rows, first_cols, col_peaks, base, factors, col_scale,
    across, spread, weights, numer,
    row_slots, col_first, col_second, core_slots, x_slots,
    src_sem, tgt_sem, row_send, row_recv, col_send, col_recv, core_send, core_recv, x_send, x_recv,
):
    ys, zs, xs, cores = dims
    tgts = xs * cores
    rows, width = src_ref.shape
    cols = tgt_ref.shape[0]
    row_tiles, col_tiles = rows // LANES, cols // LANES
    half = col_tiles // 2
    share = rows // tgts
    mine = rows // cores
    log_rows = math.log2(rows * ys * zs)
    log_cols = math.log2(cols * tgts)
    per_square = SCALE / width

    me_s, me_t = lax.axis_index("src"), lax.axis_index("tgt")
    y, z = lax.div(me_s, zs), lax.rem(me_s, zs)
    x, core = lax.div(me_t, cores), lax.rem(me_t, cores)
    other = 1 - core

    def tgt_id(dx, which):
        return (me_s, lax.rem(x + dx, xs) * cores + which)

    x_order = farthest_first(xs)
    tgt_ids = [tgt_id(dx, which) for dx in x_order for which in (other, core)] + [tgt_id(0, other)]
    y_ids = [(lax.rem(y + d, ys) * zs + z, me_t) for d in farthest_first(ys)]
    z_ids = [(y * zs + lax.rem(z + d, zs), me_t) for d in farthest_first(zs)]

    src_copy = pltpu.make_async_copy(src_hbm, src_ref, src_sem)
    src_copy.start()
    tgt_copies = []
    for j in range(cols // LOAD):
        at = pl.ds(j * LOAD, LOAD)
        tgt_copies.append(pltpu.make_async_copy(tgt_hbm.at[at], tgt_ref.at[at], tgt_sem.at[j]))
        tgt_copies[-1].start()

    barrier = pltpu.get_barrier_semaphore()
    everyone = y_ids + z_ids + tgt_ids
    for peer in everyone:
        pl.semaphore_signal(barrier, inc=1, device_id=peer, device_id_type=MESH)

    def copy_of(src, dst, send_sem, recv_sem, peer):
        return pltpu.make_async_remote_copy(
            src_ref=src, dst_ref=dst, send_sem=send_sem, recv_sem=recv_sem,
            device_id=peer, device_id_type=MESH,
        )

    def share_slot(slots, me, peers, send_sem, recv_sem):
        for peer in peers:
            copy_of(slots.at[me], slots.at[me], send_sem, recv_sem, peer).start()

    def share_both(slots, legs, send_sem, recv_sem):
        longest = max(len(peers) for _, peers in legs)
        for k in range(longest):
            for p, (me, peers) in enumerate(legs):
                if k < len(peers):
                    slot = slots.at[p, me]
                    copy_of(slot, slot, send_sem.at[p], recv_sem.at[p], peers[k]).start()

    def arrived(slots, peers, send_sem, recv_sem):
        others = slots.at[pl.ds(0, len(peers))]
        copy_of(others, others, send_sem, recv_sem, peers[0]).wait_recv()

    def sent(slots, peers, send_sem, recv_sem):
        others = slots.at[pl.ds(0, len(peers))]
        copy_of(others, others, send_sem, recv_sem, peers[0]).wait_send()

    def squares(ref, t):
        block = ref[t * LANES:(t + 1) * LANES, :].astype(jnp.float32)
        block = block * block
        part = add_up([block[:, k * LANES:(k + 1) * LANES] for k in range(width // LANES)])
        return jnp.sum(part.T, axis=0, keepdims=True) * per_square

    src_copy.wait()
    def load_body(j, carry):
        base_row = pl.multiple_of(j * LOAD, LOAD)
        at = pl.ds(base_row, LOAD)
        pltpu.make_async_copy(tgt_hbm.at[at], tgt_ref.at[at], tgt_sem.at[j]).wait()
        for i in range(LOAD // CHUNK):
            rows_at = pl.ds(pl.multiple_of(base_row + i * CHUNK, CHUNK), CHUNK)
            block = lax.dot_general(
                src_ref[...], tgt_ref[rows_at, :], (((1,), (1,)), ((), ())),
                preferred_element_type=jnp.float32,
            ) * (2.0 * per_square)
            for k in range(CHUNK // LANES):
                scores[j * (LOAD // LANES) + i * (CHUNK // LANES) + k] = block[:, k * LANES:(k + 1) * LANES]
        for k in range(LOAD // LANES):
            block = tgt_ref[pl.ds(pl.multiple_of(base_row + k * LANES, LANES), LANES), :].astype(jnp.float32)
            block = block * block
            part = add_up([block[:, q * LANES:(q + 1) * LANES] for q in range(width // LANES)])
            sq_cols[pl.ds(j * (LOAD // LANES) + k, 1), :] = jnp.sum(part.T, axis=0, keepdims=True) * per_square
        return carry

    lax.fori_loop(0, cols // LOAD, load_body, 0)

    held = [jnp.broadcast_to(sq_cols[t:t + 1, :], (SUB, LANES)) for t in range(col_tiles)]

    def first_row_body(r, carry):
        at = pl.ds(pl.multiple_of(r * SUB, SUB), SUB)
        across[at, :] = lse_of([scores[t, at, :] - held[t] for t in range(col_tiles)])
        return carry

    lax.fori_loop(0, rows // SUB, first_row_body, 0, unroll=8)
    for h in range(row_tiles):
        row_slots[0, me_t, h:h + 1, :] = lse_down(across[h * LANES:(h + 1) * LANES, :].T)

    pl.semaphore_wait(barrier, len(everyone))

    def send_rows(step):
        share_slot(row_slots.at[step], me_t, tgt_ids, row_send.at[step], row_recv.at[step])

    def rows_here(step):
        arrived(row_slots.at[step], tgt_ids, row_send.at[step], row_recv.at[step])
        return [row_slots[step, k] for k in range(tgts)]

    def spread_rows(values):
        for h in range(row_tiles):
            block = jnp.broadcast_to(values[h:h + 1, :], (LANES, LANES))
            spread[h * LANES:(h + 1) * LANES, :] = block.T

    first_leg = ((y, y_ids), (z, z_ids))
    second_leg = ((z, z_ids), (y, y_ids))

    def send_cols(step):
        share_both(col_first.at[step], first_leg, col_send.at[step, 0], col_recv.at[step, 0])

    def turn_cols(step, combine):
        for p in range(2):
            peers = first_leg[p][1]
            arrived(col_first.at[step, p], peers, col_send.at[step, 0, p], col_recv.at[step, 0, p])
            col_second[step, p, second_leg[p][0]] = combine(
                [col_first[step, p, k] for k in range(len(peers) + 1)]
            )
        share_both(col_second.at[step], second_leg, col_send.at[step, 1], col_recv.at[step, 1])

    def cols_here(step, p, combine):
        peers = second_leg[p][1]
        arrived(col_second.at[step, p], peers, col_send.at[step, 1, p], col_recv.at[step, 1, p])
        return combine([col_second[step, p, k] for k in range(len(peers) + 1)])

    def first_col_body(p):
        me = first_leg[p][0]

        def body(k, carry):
            t = p * half + k

            def term(r):
                return scores[t, r * SUB:(r + 1) * SUB, :] + spread[r * SUB:(r + 1) * SUB, :]

            peak = tree(jnp.maximum, [term(r) for r in range(rows // SUB)])
            peak = jnp.max(peak, axis=0, keepdims=True)
            sums = []
            for r in range(rows // SUB):
                value = jnp.exp2(term(r) - peak)
                scores[t, r * SUB:(r + 1) * SUB, :] = value
                sums.append(value)
            total = jnp.sum(add_up(sums), axis=0, keepdims=True)
            col_peaks[pl.ds(t, 1), :] = peak
            col_first[0, p, me, pl.ds(k, 1), :] = peak + jnp.log2(total)
            return carry

        return body

    def col_body(step, p):
        me = first_leg[p][0]

        def body(k, carry):
            t = p * half + k
            total = add_up(
                [scores[t, r * SUB:(r + 1) * SUB, :] * spread[r * SUB:(r + 1) * SUB, :]
                 for r in range(rows // SUB)]
            )
            total = jnp.sum(total, axis=0, keepdims=True) * base[pl.ds(t, 1), :]
            col_first[step, p, me, pl.ds(k, 1), :] = total
            return carry

        return body

    for step in range(ITERS):
        send_rows(step)
        if step == 0:
            potential = -log_rows - lse_of(rows_here(step))
            first_rows[...] = potential
            spread_rows(potential)
        else:
            scale = 1.0 / (add_up(rows_here(step)) * (2.0 ** log_rows))
            spread_rows(scale)
        for p in range(2):
            body = col_body(step, p) if step else first_col_body(p)
            lax.fori_loop(0, half, body, 0, unroll=8 if step else 4)
        send_cols(step)
        if step == 0:
            for h in range(row_tiles):
                sq_rows[h:h + 1, :] = squares(src_ref, h)
        if step == ITERS - 1:
            final = first_rows[...] + (jnp.log2(scale) if step else 0.0) + sq_rows[...]
            rows_ref[...] = final * (1.0 / SCALE)
        combine = add_up if step else lse_of
        turn_cols(step, combine)
        for p in range(2):
            at = slice(p * half, (p + 1) * half)
            total = cols_here(step, p, combine)
            if step == 0:
                potential = -log_cols - total
                first_cols[at, :] = potential
                base[at, :] = jnp.exp2(col_peaks[at, :] + potential)
                factors[at, :] = base[at, :]
            else:
                scale = 1.0 / (total * (2.0 ** log_cols))
                factors[at, :] = base[at, :] * scale
                col_scale[at, :] = scale
            if step < ITERS - 1:
                held = [
                    jnp.broadcast_to(factors[p * half + k:p * half + k + 1, :], (SUB, LANES))
                    for k in range(half)
                ]

                def row_body(r, carry, p=p, held=held):
                    at = pl.ds(pl.multiple_of(r * SUB, SUB), SUB)
                    terms = [scores[p * half + k, at, :] * held[k] for k in range(half)]
                    if p:
                        terms.append(across[at, :])
                    across[at, :] = add_up(terms)
                    return carry

                lax.fori_loop(0, rows // SUB, row_body, 0, unroll=8)
        if step < ITERS - 1:
            for h in range(row_tiles):
                total = jnp.sum(across[h * LANES:(h + 1) * LANES, :].T, axis=0, keepdims=True)
                row_slots[step + 1, me_t, h:h + 1, :] = total

    tall = 2 * SUB

    def weight_body(b, carry):
        place = lax.div(b * tall, share)
        within = lax.rem(b * tall, share)
        which = lax.rem(other + lax.div(place, xs), cores)
        start = (lax.rem(place, xs) * cores + which) * share + within
        at = pl.ds(pl.multiple_of(start, tall), tall)
        to = pl.ds(pl.multiple_of(b * tall, tall), tall)
        values = [scores[t, at, :] * factors[t:t + 1, :] for t in range(col_tiles)]
        for t in range(col_tiles):
            weights[to, t * LANES:(t + 1) * LANES] = values[t].astype(jnp.bfloat16)
        across[at, :] = add_up(values)
        return carry

    lax.fori_loop(0, rows // tall, weight_body, 0, unroll=4)
    chunks = width // CHUNK
    sibling = tgt_id(0, other)

    def core_copy(n):
        return copy_of(
            numer.at[n, pl.ds(0, mine)], core_slots.at[n], core_send.at[n], core_recv.at[n], sibling
        )

    for n in range(chunks):
        numer[n] = jnp.dot(
            weights[...], tgt_ref[:, n * CHUNK:(n + 1) * CHUNK], preferred_element_type=jnp.float32
        )
        core_copy(n).start()
    for h in range(row_tiles):
        total = jnp.sum(across[h * LANES:(h + 1) * LANES, :].T, axis=0, keepdims=True)
        row_slots[ITERS, me_t, h:h + 1, :] = total
    send_rows(ITERS)

    def x_part(n, dx):
        place = lax.rem(x + dx, xs) * share
        return (
            pl.ds(pl.multiple_of(mine + place, share), share),
            pl.ds(pl.multiple_of(place, share), share),
        )

    for n in range(chunks):
        core_copy(n).wait_recv()
        for k, dx in enumerate(x_order):
            own, got = x_part(n, dx)
            numer[n, own, :] = numer[n, own, :] + core_slots[n, got, :]
            copy_of(
                numer.at[n, own], x_slots.at[n, k], x_send.at[n], x_recv.at[n], tgt_id(dx, core)
            ).start()

    final = first_cols[...] + jnp.log2(col_scale[...]) + sq_cols[...]
    cols_ref[...] = final * (1.0 / SCALE)
    spread_rows(1.0 / add_up(rows_here(ITERS)))
    scale = spread[pl.ds(pl.multiple_of(me_t * share, share), share), :]

    def x_wait(n):
        return copy_of(x_slots.at[n], x_slots.at[n], x_send.at[n], x_recv.at[n], sibling)

    for n in range(chunks):
        own, got = x_part(n, 0)
        near = numer[n, own, :] + core_slots[n, got, :]
        x_wait(n).wait_recv()
        total = near + add_up([x_slots[n, k] for k in range(xs - 1)])
        for k in range(CHUNK // LANES):
            piece = total[:, k * LANES:(k + 1) * LANES] * scale
            start = n * CHUNK + k * LANES
            bary_ref[:, start:start + LANES] = piece.astype(jnp.bfloat16)

    for step in range(ITERS + 1):
        sent(row_slots.at[step], tgt_ids, row_send.at[step], row_recv.at[step])
    for step in range(ITERS):
        for p in range(2):
            for leg, slots, plan in ((0, col_first, first_leg), (1, col_second, second_leg)):
                sent(
                    slots.at[step, p], plan[p][1], col_send.at[step, leg, p], col_recv.at[step, leg, p]
                )
    for n in range(chunks):
        core_copy(n).wait_send()
        x_wait(n).wait_send()


def emit(bary, rows, cols, bary_out, rows_out, cols_out, sems):
    copies = [
        pltpu.make_async_copy(held, out, sems.at[k])
        for k, (held, out) in enumerate(((bary, bary_out), (rows, rows_out), (cols, cols_out)))
    ]
    for copy in copies:
        copy.start()
    for copy in copies:
        copy.wait()


def build(mesh, dims):
    ys, zs, xs, cores = dims
    tgts = xs * cores
    most = max(ys, zs)

    def on_device(sources, targets):
        rows, width = sources.shape
        cols = targets.shape[0]
        row_tiles, col_tiles = rows // LANES, cols // LANES
        half, share, chunks = col_tiles // 2, rows // tgts, width // CHUNK
        f32 = jnp.float32
        dma = pltpu.SemaphoreType.DMA
        bary, dual_rows, dual_cols = pl.pallas_call(
            functools.partial(kernel, dims),
            out_shape=(
                jax.ShapeDtypeStruct((share, width), jnp.bfloat16),
                jax.ShapeDtypeStruct((row_tiles, LANES), f32),
                jax.ShapeDtypeStruct((col_tiles, LANES), f32),
            ),
            in_specs=[pl.BlockSpec(memory_space=pl.ANY)] * 2,
            out_specs=[pl.BlockSpec(memory_space=pltpu.VMEM)] * 3,
            scratch_shapes=[
                pltpu.VMEM((rows, width), jnp.bfloat16),
                pltpu.VMEM((cols, width), jnp.bfloat16),
                pltpu.VMEM((col_tiles, rows, LANES), f32),
                pltpu.VMEM((row_tiles, LANES), f32),
                pltpu.VMEM((col_tiles, LANES), f32),
                pltpu.VMEM((row_tiles, LANES), f32),
                pltpu.VMEM((col_tiles, LANES), f32),
                pltpu.VMEM((col_tiles, LANES), f32),
                pltpu.VMEM((col_tiles, LANES), f32),
                pltpu.VMEM((col_tiles, LANES), f32),
                pltpu.VMEM((col_tiles, LANES), f32),
                pltpu.VMEM((rows, LANES), f32),
                pltpu.VMEM((rows, LANES), f32),
                pltpu.VMEM((rows, cols), jnp.bfloat16),
                pltpu.VMEM((chunks, rows, CHUNK), f32),
                pltpu.VMEM((ITERS + 1, tgts, row_tiles, LANES), f32),
                pltpu.VMEM((ITERS, 2, most, half, LANES), f32),
                pltpu.VMEM((ITERS, 2, most, half, LANES), f32),
                pltpu.VMEM((chunks, rows // cores, CHUNK), f32),
                pltpu.VMEM((chunks, xs - 1, share, CHUNK), f32),
                dma,
                dma((cols // LOAD,)),
                dma((ITERS + 1,)),
                dma((ITERS + 1,)),
                dma((ITERS, 2, 2)),
                dma((ITERS, 2, 2)),
                dma((chunks,)),
                dma((chunks,)),
                dma((chunks,)),
                dma((chunks,)),
            ],
            compiler_params=pltpu.CompilerParams(
                collective_id=0, has_side_effects=True, vmem_limit_bytes=VMEM_GRANT
            ),
        )(sources, targets)
        bary, dual_rows, dual_cols = pl.pallas_call(
            emit,
            out_shape=(
                jax.ShapeDtypeStruct(bary.shape, bary.dtype),
                jax.ShapeDtypeStruct(dual_rows.shape, f32),
                jax.ShapeDtypeStruct(dual_cols.shape, f32),
            ),
            in_specs=[pl.BlockSpec(memory_space=pl.ANY)] * 3,
            out_specs=[pl.BlockSpec(memory_space=pl.ANY)] * 3,
            scratch_shapes=[dma((3,))],
            compiler_params=pltpu.CompilerParams(vmem_limit_bytes=1024 * 1024),
        )(bary, dual_rows, dual_cols)
        return bary, dual_rows.reshape(rows), dual_cols.reshape(cols)

    in_specs = (P("src", None), P("tgt", None))
    out_specs = (P(("src", "tgt"), None), P("src"), P("tgt"))
    return jax.shard_map(
        on_device, mesh=mesh, in_specs=in_specs, out_specs=out_specs, check_vma=False
    )


def solution(mesh):
    return build(mesh, (8, 8, 4, 2))
```

```python
import functools
import math

import jax
import jax.numpy as jnp
from jax import lax
from jax.experimental import pallas as pl
from jax.experimental.pallas import tpu as pltpu
from jax.sharding import PartitionSpec as P

ITERS = 3
ENTROPY = 0.02
SCALE = math.log2(math.e) / ENTROPY
LANES = 128
SUB = 8
CHUNK = 256
LOAD = 1024
VMEM_GRANT = 55040 * 1024
MESH = pl.DeviceIdType.MESH


def tree(op, items):
    items = list(items)
    while len(items) > 1:
        paired = [op(items[k], items[k + 1]) for k in range(0, len(items) - 1, 2)]
        if len(items) % 2:
            paired.append(items[-1])
        items = paired
    return items[0]


def add_up(items):
    return tree(jnp.add, items)


def lse_of(parts):
    peak = tree(jnp.maximum, parts)
    return peak + jnp.log2(add_up([jnp.exp2(part - peak) for part in parts]))


def lse_down(block):
    peak = jnp.max(block, axis=0, keepdims=True)
    return peak + jnp.log2(jnp.sum(jnp.exp2(block - peak), axis=0, keepdims=True))


def farthest_first(n):
    return sorted(range(1, n), key=lambda d: -min(d, n - d))


def kernel(
    dims, src_hbm, tgt_hbm, bary_ref, rows_ref, cols_ref,
    src_ref, tgt_ref, scores, sq_rows, sq_cols, first_rows, first_cols, col_peaks, base, factors, col_scale,
    across, spread, weights, numer,
    row_slots, col_first, col_second, core_slots, x_slots,
    src_sem, tgt_sem, row_send, row_recv, col_send, col_recv, core_send, core_recv, x_send, x_recv,
):
    ys, zs, xs, cores = dims
    tgts = xs * cores
    rows, width = src_ref.shape
    cols = tgt_ref.shape[0]
    row_tiles, col_tiles = rows // LANES, cols // LANES
    half = col_tiles // 2
    share = rows // tgts
    mine = rows // cores
    log_rows = math.log2(rows * ys * zs)
    log_cols = math.log2(cols * tgts)
    per_square = SCALE / width

    me_s, me_t = lax.axis_index("src"), lax.axis_index("tgt")
    y, z = lax.div(me_s, zs), lax.rem(me_s, zs)
    x, core = lax.div(me_t, cores), lax.rem(me_t, cores)
    other = 1 - core

    def tgt_id(dx, which):
        return (me_s, lax.rem(x + dx, xs) * cores + which)

    x_order = farthest_first(xs)
    tgt_ids = [tgt_id(dx, which) for dx in x_order for which in (other, core)] + [tgt_id(0, other)]
    y_ids = [(lax.rem(y + d, ys) * zs + z, me_t) for d in farthest_first(ys)]
    z_ids = [(y * zs + lax.rem(z + d, zs), me_t) for d in farthest_first(zs)]

    src_copy = pltpu.make_async_copy(src_hbm, src_ref, src_sem)
    src_copy.start()
    tgt_copies = []
    for j in range(cols // LOAD):
        at = pl.ds(j * LOAD, LOAD)
        tgt_copies.append(pltpu.make_async_copy(tgt_hbm.at[at], tgt_ref.at[at], tgt_sem.at[j]))
        tgt_copies[-1].start()

    barrier = pltpu.get_barrier_semaphore()
    everyone = y_ids + z_ids + tgt_ids
    for peer in everyone:
        pl.semaphore_signal(barrier, inc=1, device_id=peer, device_id_type=MESH)

    def copy_of(src, dst, send_sem, recv_sem, peer):
        return pltpu.make_async_remote_copy(
            src_ref=src, dst_ref=dst, send_sem=send_sem, recv_sem=recv_sem,
            device_id=peer, device_id_type=MESH,
        )

    def share_slot(slots, me, peers, send_sem, recv_sem):
        for peer in peers:
            copy_of(slots.at[me], slots.at[me], send_sem, recv_sem, peer).start()

    def share_both(slots, legs, send_sem, recv_sem):
        longest = max(len(peers) for _, peers in legs)
        for k in range(longest):
            for p, (me, peers) in enumerate(legs):
                if k < len(peers):
                    slot = slots.at[p, me]
                    copy_of(slot, slot, send_sem.at[p], recv_sem.at[p], peers[k]).start()

    def arrived(slots, peers, send_sem, recv_sem):
        others = slots.at[pl.ds(0, len(peers))]
        copy_of(others, others, send_sem, recv_sem, peers[0]).wait_recv()

    def sent(slots, peers, send_sem, recv_sem):
        others = slots.at[pl.ds(0, len(peers))]
        copy_of(others, others, send_sem, recv_sem, peers[0]).wait_send()

    def squares(ref, t):
        block = ref[t * LANES:(t + 1) * LANES, :].astype(jnp.float32)
        block = block * block
        part = add_up([block[:, k * LANES:(k + 1) * LANES] for k in range(width // LANES)])
        return jnp.sum(part.T, axis=0, keepdims=True) * per_square

    src_copy.wait()
    def load_body(j, carry):
        base_row = pl.multiple_of(j * LOAD, LOAD)
        at = pl.ds(base_row, LOAD)
        pltpu.make_async_copy(tgt_hbm.at[at], tgt_ref.at[at], tgt_sem.at[j]).wait()
        for i in range(LOAD // CHUNK):
            rows_at = pl.ds(pl.multiple_of(base_row + i * CHUNK, CHUNK), CHUNK)
            block = lax.dot_general(
                src_ref[...], tgt_ref[rows_at, :], (((1,), (1,)), ((), ())),
                preferred_element_type=jnp.float32,
            ) * (2.0 * per_square)
            for k in range(CHUNK // LANES):
                scores[j * (LOAD // LANES) + i * (CHUNK // LANES) + k] = block[:, k * LANES:(k + 1) * LANES]
        for k in range(LOAD // LANES):
            block = tgt_ref[pl.ds(pl.multiple_of(base_row + k * LANES, LANES), LANES), :].astype(jnp.float32)
            block = block * block
            part = add_up([block[:, q * LANES:(q + 1) * LANES] for q in range(width // LANES)])
            sq_cols[pl.ds(j * (LOAD // LANES) + k, 1), :] = jnp.sum(part.T, axis=0, keepdims=True) * per_square
        tiles = LOAD // LANES
        held = [
            jnp.broadcast_to(sq_cols[pl.ds(j * tiles + k, 1), :], (SUB, LANES)) for k in range(tiles)
        ]

        def first_row_body(r, inner):
            at = pl.ds(pl.multiple_of(r * SUB, SUB), SUB)
            part = lse_of([scores[j * tiles + k, at, :] - held[k] for k in range(tiles)])
            numer[j, at, :LANES] = part
            return inner

        lax.fori_loop(0, rows // SUB, first_row_body, 0, unroll=8)
        return carry

    lax.fori_loop(0, cols // LOAD, load_body, 0)

    across[...] = lse_of([numer[j, :, :LANES] for j in range(cols // LOAD)])
    for h in range(row_tiles):
        row_slots[0, me_t, h:h + 1, :] = lse_down(across[h * LANES:(h + 1) * LANES, :].T)

    pl.semaphore_wait(barrier, len(everyone))

    def send_rows(step):
        share_slot(row_slots.at[step], me_t, tgt_ids, row_send.at[step], row_recv.at[step])

    def rows_here(step):
        arrived(row_slots.at[step], tgt_ids, row_send.at[step], row_recv.at[step])
        return [row_slots[step, k] for k in range(tgts)]

    def spread_rows(values):
        for h in range(row_tiles):
            block = jnp.broadcast_to(values[h:h + 1, :], (LANES, LANES))
            spread[h * LANES:(h + 1) * LANES, :] = block.T

    first_leg = ((y, y_ids), (z, z_ids))
    second_leg = ((z, z_ids), (y, y_ids))

    def send_cols(step):
        share_both(col_first.at[step], first_leg, col_send.at[step, 0], col_recv.at[step, 0])

    def turn_cols(step, combine):
        for p in range(2):
            peers = first_leg[p][1]
            arrived(col_first.at[step, p], peers, col_send.at[step, 0, p], col_recv.at[step, 0, p])
            col_second[step, p, second_leg[p][0]] = combine(
                [col_first[step, p, k] for k in range(len(peers) + 1)]
            )
        share_both(col_second.at[step], second_leg, col_send.at[step, 1], col_recv.at[step, 1])

    def cols_here(step, p, combine):
        peers = second_leg[p][1]
        arrived(col_second.at[step, p], peers, col_send.at[step, 1, p], col_recv.at[step, 1, p])
        return combine([col_second[step, p, k] for k in range(len(peers) + 1)])

    def first_col_body(p):
        me = first_leg[p][0]

        def body(k, carry):
            t = p * half + k

            def term(r):
                return scores[t, r * SUB:(r + 1) * SUB, :] + spread[r * SUB:(r + 1) * SUB, :]

            peak = tree(jnp.maximum, [term(r) for r in range(rows // SUB)])
            peak = jnp.max(peak, axis=0, keepdims=True)
            sums = []
            for r in range(rows // SUB):
                value = jnp.exp2(term(r) - peak)
                scores[t, r * SUB:(r + 1) * SUB, :] = value
                sums.append(value)
            total = jnp.sum(add_up(sums), axis=0, keepdims=True)
            col_peaks[pl.ds(t, 1), :] = peak
            col_first[0, p, me, pl.ds(k, 1), :] = peak + jnp.log2(total)
            return carry

        return body

    def col_body(step, p):
        me = first_leg[p][0]

        def body(k, carry):
            t = p * half + k
            total = add_up(
                [scores[t, r * SUB:(r + 1) * SUB, :] * spread[r * SUB:(r + 1) * SUB, :]
                 for r in range(rows // SUB)]
            )
            total = jnp.sum(total, axis=0, keepdims=True) * base[pl.ds(t, 1), :]
            col_first[step, p, me, pl.ds(k, 1), :] = total
            return carry

        return body

    for step in range(ITERS):
        send_rows(step)
        if step == 0:
            potential = -log_rows - lse_of(rows_here(step))
            first_rows[...] = potential
            spread_rows(potential)
        else:
            scale = 1.0 / (add_up(rows_here(step)) * (2.0 ** log_rows))
            spread_rows(scale)
        for p in range(2):
            body = col_body(step, p) if step else first_col_body(p)
            lax.fori_loop(0, half, body, 0, unroll=8 if step else 4)
        send_cols(step)
        if step == 0:
            for h in range(row_tiles):
                sq_rows[h:h + 1, :] = squares(src_ref, h)
        if step == ITERS - 1:
            final = first_rows[...] + (jnp.log2(scale) if step else 0.0) + sq_rows[...]
            rows_ref[...] = final * (1.0 / SCALE)
        combine = add_up if step else lse_of
        turn_cols(step, combine)
        for p in range(2):
            at = slice(p * half, (p + 1) * half)
            total = cols_here(step, p, combine)
            if step == 0:
                potential = -log_cols - total
                first_cols[at, :] = potential
                base[at, :] = jnp.exp2(col_peaks[at, :] + potential)
                factors[at, :] = base[at, :]
            else:
                scale = 1.0 / (total * (2.0 ** log_cols))
                factors[at, :] = base[at, :] * scale
                col_scale[at, :] = scale
            if step < ITERS - 1:
                held = [
                    jnp.broadcast_to(factors[p * half + k:p * half + k + 1, :], (SUB, LANES))
                    for k in range(half)
                ]

                def row_body(r, carry, p=p, held=held):
                    at = pl.ds(pl.multiple_of(r * SUB, SUB), SUB)
                    terms = [scores[p * half + k, at, :] * held[k] for k in range(half)]
                    if p:
                        terms.append(across[at, :])
                    across[at, :] = add_up(terms)
                    return carry

                lax.fori_loop(0, rows // SUB, row_body, 0, unroll=8)
        if step < ITERS - 1:
            for h in range(row_tiles):
                total = jnp.sum(across[h * LANES:(h + 1) * LANES, :].T, axis=0, keepdims=True)
                row_slots[step + 1, me_t, h:h + 1, :] = total

    tall = 2 * SUB

    def weight_body(b, carry):
        place = lax.div(b * tall, share)
        within = lax.rem(b * tall, share)
        which = lax.rem(other + lax.div(place, xs), cores)
        start = (lax.rem(place, xs) * cores + which) * share + within
        at = pl.ds(pl.multiple_of(start, tall), tall)
        to = pl.ds(pl.multiple_of(b * tall, tall), tall)
        values = [scores[t, at, :] * factors[t:t + 1, :] for t in range(col_tiles)]
        for t in range(col_tiles):
            weights[to, t * LANES:(t + 1) * LANES] = values[t].astype(jnp.bfloat16)
        across[at, :] = add_up(values)
        return carry

    lax.fori_loop(0, rows // tall, weight_body, 0, unroll=4)
    chunks = width // CHUNK
    sibling = tgt_id(0, other)

    def core_copy(n):
        return copy_of(
            numer.at[n, pl.ds(0, mine)], core_slots.at[n], core_send.at[n], core_recv.at[n], sibling
        )

    for n in range(chunks):
        numer[n] = jnp.dot(
            weights[...], tgt_ref[:, n * CHUNK:(n + 1) * CHUNK], preferred_element_type=jnp.float32
        )
        core_copy(n).start()
    for h in range(row_tiles):
        total = jnp.sum(across[h * LANES:(h + 1) * LANES, :].T, axis=0, keepdims=True)
        row_slots[ITERS, me_t, h:h + 1, :] = total
    send_rows(ITERS)

    def x_part(n, dx):
        place = lax.rem(x + dx, xs) * share
        return (
            pl.ds(pl.multiple_of(mine + place, share), share),
            pl.ds(pl.multiple_of(place, share), share),
        )

    for n in range(chunks):
        core_copy(n).wait_recv()
        for k, dx in enumerate(x_order):
            own, got = x_part(n, dx)
            numer[n, own, :] = numer[n, own, :] + core_slots[n, got, :]
            copy_of(
                numer.at[n, own], x_slots.at[n, k], x_send.at[n], x_recv.at[n], tgt_id(dx, core)
            ).start()

    final = first_cols[...] + jnp.log2(col_scale[...]) + sq_cols[...]
    cols_ref[...] = final * (1.0 / SCALE)
    spread_rows(1.0 / add_up(rows_here(ITERS)))
    scale = spread[pl.ds(pl.multiple_of(me_t * share, share), share), :]

    def x_wait(n):
        return copy_of(x_slots.at[n], x_slots.at[n], x_send.at[n], x_recv.at[n], sibling)

    for step in range(ITERS + 1):
        sent(row_slots.at[step], tgt_ids, row_send.at[step], row_recv.at[step])
    for step in range(ITERS):
        for p in range(2):
            for leg, slots, plan in ((0, col_first, first_leg), (1, col_second, second_leg)):
                sent(
                    slots.at[step, p], plan[p][1], col_send.at[step, leg, p], col_recv.at[step, leg, p]
                )
    for n in range(chunks):
        core_copy(n).wait_send()

    for n in range(chunks):
        own, got = x_part(n, 0)
        near = numer[n, own, :] + core_slots[n, got, :]
        x_wait(n).wait_recv()
        total = near + add_up([x_slots[n, k] for k in range(xs - 1)])
        for k in range(CHUNK // LANES):
            piece = total[:, k * LANES:(k + 1) * LANES] * scale
            start = n * CHUNK + k * LANES
            bary_ref[:, start:start + LANES] = piece.astype(jnp.bfloat16)

    for n in range(chunks):
        x_wait(n).wait_send()


def emit(bary, rows, cols, bary_out, rows_out, cols_out, sems):
    copies = [
        pltpu.make_async_copy(held, out, sems.at[k])
        for k, (held, out) in enumerate(((bary, bary_out), (rows, rows_out), (cols, cols_out)))
    ]
    for copy in copies:
        copy.start()
    for copy in copies:
        copy.wait()


def build(mesh, dims):
    ys, zs, xs, cores = dims
    tgts = xs * cores
    most = max(ys, zs)

    def on_device(sources, targets):
        rows, width = sources.shape
        cols = targets.shape[0]
        row_tiles, col_tiles = rows // LANES, cols // LANES
        half, share, chunks = col_tiles // 2, rows // tgts, width // CHUNK
        f32 = jnp.float32
        dma = pltpu.SemaphoreType.DMA
        bary, dual_rows, dual_cols = pl.pallas_call(
            functools.partial(kernel, dims),
            out_shape=(
                jax.ShapeDtypeStruct((share, width), jnp.bfloat16),
                jax.ShapeDtypeStruct((row_tiles, LANES), f32),
                jax.ShapeDtypeStruct((col_tiles, LANES), f32),
            ),
            in_specs=[pl.BlockSpec(memory_space=pl.ANY)] * 2,
            out_specs=[pl.BlockSpec(memory_space=pltpu.VMEM)] * 3,
            scratch_shapes=[
                pltpu.VMEM((rows, width), jnp.bfloat16),
                pltpu.VMEM((cols, width), jnp.bfloat16),
                pltpu.VMEM((col_tiles, rows, LANES), f32),
                pltpu.VMEM((row_tiles, LANES), f32),
                pltpu.VMEM((col_tiles, LANES), f32),
                pltpu.VMEM((row_tiles, LANES), f32),
                pltpu.VMEM((col_tiles, LANES), f32),
                pltpu.VMEM((col_tiles, LANES), f32),
                pltpu.VMEM((col_tiles, LANES), f32),
                pltpu.VMEM((col_tiles, LANES), f32),
                pltpu.VMEM((col_tiles, LANES), f32),
                pltpu.VMEM((rows, LANES), f32),
                pltpu.VMEM((rows, LANES), f32),
                pltpu.VMEM((rows, cols), jnp.bfloat16),
                pltpu.VMEM((chunks, rows, CHUNK), f32),
                pltpu.VMEM((ITERS + 1, tgts, row_tiles, LANES), f32),
                pltpu.VMEM((ITERS, 2, most, half, LANES), f32),
                pltpu.VMEM((ITERS, 2, most, half, LANES), f32),
                pltpu.VMEM((chunks, rows // cores, CHUNK), f32),
                pltpu.VMEM((chunks, xs - 1, share, CHUNK), f32),
                dma,
                dma((cols // LOAD,)),
                dma((ITERS + 1,)),
                dma((ITERS + 1,)),
                dma((ITERS, 2, 2)),
                dma((ITERS, 2, 2)),
                dma((chunks,)),
                dma((chunks,)),
                dma((chunks,)),
                dma((chunks,)),
            ],
            compiler_params=pltpu.CompilerParams(
                collective_id=0, has_side_effects=True, vmem_limit_bytes=VMEM_GRANT
            ),
        )(sources, targets)
        bary, dual_rows, dual_cols = pl.pallas_call(
            emit,
            out_shape=(
                jax.ShapeDtypeStruct(bary.shape, bary.dtype),
                jax.ShapeDtypeStruct(dual_rows.shape, f32),
                jax.ShapeDtypeStruct(dual_cols.shape, f32),
            ),
            in_specs=[pl.BlockSpec(memory_space=pl.ANY)] * 3,
            out_specs=[pl.BlockSpec(memory_space=pl.ANY)] * 3,
            scratch_shapes=[dma((3,))],
            compiler_params=pltpu.CompilerParams(vmem_limit_bytes=1024 * 1024),
        )(bary, dual_rows, dual_cols)
        return bary, dual_rows.reshape(rows), dual_cols.reshape(cols)

    in_specs = (P("src", None), P("tgt", None))
    out_specs = (P(("src", "tgt"), None), P("src"), P("tgt"))
    return jax.shard_map(
        on_device, mesh=mesh, in_specs=in_specs, out_specs=out_specs, check_vma=False
    )


def solution(mesh):
    return build(mesh, (8, 8, 4, 2))
```

```python
import functools
import math

import jax
import jax.numpy as jnp
from jax import lax
from jax.experimental import pallas as pl
from jax.experimental.pallas import tpu as pltpu
from jax.sharding import PartitionSpec as P

ITERS = 3
ENTROPY = 0.02
SCALE = math.log2(math.e) / ENTROPY
LANES = 128
SUB = 8
CHUNK = 256
LOAD = 1024
VMEM_GRANT = 55040 * 1024
MESH = pl.DeviceIdType.MESH


def tree(op, items):
    items = list(items)
    while len(items) > 1:
        paired = [op(items[k], items[k + 1]) for k in range(0, len(items) - 1, 2)]
        if len(items) % 2:
            paired.append(items[-1])
        items = paired
    return items[0]


def add_up(items):
    return tree(jnp.add, items)


def lse_of(parts):
    peak = tree(jnp.maximum, parts)
    return peak + jnp.log2(add_up([jnp.exp2(part - peak) for part in parts]))


def lse_down(block):
    peak = jnp.max(block, axis=0, keepdims=True)
    return peak + jnp.log2(jnp.sum(jnp.exp2(block - peak), axis=0, keepdims=True))


def farthest_first(n):
    return sorted(range(1, n), key=lambda d: -min(d, n - d))


def kernel(
    dims, src_hbm, tgt_hbm, bary_ref, rows_ref, cols_ref,
    src_ref, tgt_ref, scores, sq_rows, sq_cols, first_rows, first_cols, col_peaks, base, factors, col_scale,
    across, spread, weights, numer,
    row_slots, col_first, col_second, core_slots, x_slots,
    src_sem, tgt_sem, row_send, row_recv, col_send, col_recv, core_send, core_recv, x_send, x_recv,
):
    ys, zs, xs, cores = dims
    tgts = xs * cores
    rows, width = src_ref.shape
    cols = tgt_ref.shape[0]
    row_tiles, col_tiles = rows // LANES, cols // LANES
    half = col_tiles // 2
    share = rows // tgts
    mine = rows // cores
    log_rows = math.log2(rows * ys * zs)
    log_cols = math.log2(cols * tgts)
    per_square = SCALE / width

    me_s, me_t = lax.axis_index("src"), lax.axis_index("tgt")
    y, z = lax.div(me_s, zs), lax.rem(me_s, zs)
    x, core = lax.div(me_t, cores), lax.rem(me_t, cores)
    other = 1 - core

    def tgt_id(dx, which):
        return (me_s, lax.rem(x + dx, xs) * cores + which)

    x_order = farthest_first(xs)
    tgt_ids = [tgt_id(dx, which) for dx in x_order for which in (other, core)] + [tgt_id(0, other)]
    y_ids = [(lax.rem(y + d, ys) * zs + z, me_t) for d in farthest_first(ys)]
    z_ids = [(y * zs + lax.rem(z + d, zs), me_t) for d in farthest_first(zs)]

    src_copy = pltpu.make_async_copy(src_hbm, src_ref, src_sem)
    src_copy.start()
    tgt_copies = []
    for j in range(cols // LOAD):
        at = pl.ds(j * LOAD, LOAD)
        tgt_copies.append(pltpu.make_async_copy(tgt_hbm.at[at], tgt_ref.at[at], tgt_sem.at[j]))
        tgt_copies[-1].start()

    barrier = pltpu.get_barrier_semaphore()
    everyone = y_ids + z_ids + tgt_ids
    for peer in everyone:
        pl.semaphore_signal(barrier, inc=1, device_id=peer, device_id_type=MESH)

    def copy_of(src, dst, send_sem, recv_sem, peer):
        return pltpu.make_async_remote_copy(
            src_ref=src, dst_ref=dst, send_sem=send_sem, recv_sem=recv_sem,
            device_id=peer, device_id_type=MESH,
        )

    def share_slot(slots, me, peers, send_sem, recv_sem):
        for peer in peers:
            copy_of(slots.at[me], slots.at[me], send_sem, recv_sem, peer).start()

    def share_both(slots, legs, send_sem, recv_sem):
        longest = max(len(peers) for _, peers in legs)
        for k in range(longest):
            for p, (me, peers) in enumerate(legs):
                if k < len(peers):
                    slot = slots.at[p, me]
                    copy_of(slot, slot, send_sem.at[p], recv_sem.at[p], peers[k]).start()

    def arrived(slots, peers, send_sem, recv_sem):
        others = slots.at[pl.ds(0, len(peers))]
        copy_of(others, others, send_sem, recv_sem, peers[0]).wait_recv()

    def sent(slots, peers, send_sem, recv_sem):
        others = slots.at[pl.ds(0, len(peers))]
        copy_of(others, others, send_sem, recv_sem, peers[0]).wait_send()

    def squares(ref, t):
        block = ref[t * LANES:(t + 1) * LANES, :].astype(jnp.float32)
        block = block * block
        part = add_up([block[:, k * LANES:(k + 1) * LANES] for k in range(width // LANES)])
        return jnp.sum(part.T, axis=0, keepdims=True) * per_square

    src_copy.wait()
    def load_body(j, carry):
        base_row = pl.multiple_of(j * LOAD, LOAD)
        at = pl.ds(base_row, LOAD)
        pltpu.make_async_copy(tgt_hbm.at[at], tgt_ref.at[at], tgt_sem.at[j]).wait()
        for i in range(LOAD // CHUNK):
            rows_at = pl.ds(pl.multiple_of(base_row + i * CHUNK, CHUNK), CHUNK)
            block = lax.dot_general(
                src_ref[...], tgt_ref[rows_at, :], (((1,), (1,)), ((), ())),
                preferred_element_type=jnp.float32,
            ) * (2.0 * per_square)
            for k in range(CHUNK // LANES):
                scores[j * (LOAD // LANES) + i * (CHUNK // LANES) + k] = block[:, k * LANES:(k + 1) * LANES]
        for k in range(LOAD // LANES):
            block = tgt_ref[pl.ds(pl.multiple_of(base_row + k * LANES, LANES), LANES), :].astype(jnp.float32)
            block = block * block
            part = add_up([block[:, q * LANES:(q + 1) * LANES] for q in range(width // LANES)])
            sq_cols[pl.ds(j * (LOAD // LANES) + k, 1), :] = jnp.sum(part.T, axis=0, keepdims=True) * per_square
        return carry

    lax.fori_loop(0, cols // LOAD, load_body, 0)

    held = [jnp.broadcast_to(sq_cols[t:t + 1, :], (SUB, LANES)) for t in range(col_tiles)]

    def first_row_body(r, carry):
        at = pl.ds(pl.multiple_of(r * SUB, SUB), SUB)
        across[at, :] = lse_of([scores[t, at, :] - held[t] for t in range(col_tiles)])
        return carry

    lax.fori_loop(0, rows // SUB, first_row_body, 0, unroll=8)
    for h in range(row_tiles):
        row_slots[0, me_t, h:h + 1, :] = lse_down(across[h * LANES:(h + 1) * LANES, :].T)

    pl.semaphore_wait(barrier, len(everyone))

    def send_rows(step):
        share_slot(row_slots.at[step], me_t, tgt_ids, row_send.at[step], row_recv.at[step])

    def rows_here(step):
        arrived(row_slots.at[step], tgt_ids, row_send.at[step], row_recv.at[step])
        return [row_slots[step, k] for k in range(tgts)]

    def spread_rows(values):
        for h in range(row_tiles):
            block = jnp.broadcast_to(values[h:h + 1, :], (LANES, LANES))
            spread[h * LANES:(h + 1) * LANES, :] = block.T

    first_leg = ((y, y_ids), (z, z_ids))
    second_leg = ((z, z_ids), (y, y_ids))

    def send_cols(step):
        share_both(col_first.at[step], first_leg, col_send.at[step, 0], col_recv.at[step, 0])

    def turn_cols(step, combine):
        for p in range(2):
            peers = first_leg[p][1]
            arrived(col_first.at[step, p], peers, col_send.at[step, 0, p], col_recv.at[step, 0, p])
            col_second[step, p, second_leg[p][0]] = combine(
                [col_first[step, p, k] for k in range(len(peers) + 1)]
            )
        share_both(col_second.at[step], second_leg, col_send.at[step, 1], col_recv.at[step, 1])

    def cols_here(step, p, combine):
        peers = second_leg[p][1]
        arrived(col_second.at[step, p], peers, col_send.at[step, 1, p], col_recv.at[step, 1, p])
        return combine([col_second[step, p, k] for k in range(len(peers) + 1)])

    def first_col_body(p):
        me = first_leg[p][0]

        def body(k, carry):
            t = p * half + k

            def term(r):
                return scores[t, r * SUB:(r + 1) * SUB, :] + spread[r * SUB:(r + 1) * SUB, :]

            peak = tree(jnp.maximum, [term(r) for r in range(rows // SUB)])
            peak = jnp.max(peak, axis=0, keepdims=True)
            sums = []
            for r in range(rows // SUB):
                value = jnp.exp2(term(r) - peak)
                scores[t, r * SUB:(r + 1) * SUB, :] = value
                sums.append(value)
            total = jnp.sum(add_up(sums), axis=0, keepdims=True)
            col_peaks[pl.ds(t, 1), :] = peak
            col_first[0, p, me, pl.ds(k, 1), :] = peak + jnp.log2(total)
            return carry

        return body

    def col_body(step, p):
        me = first_leg[p][0]

        def body(k, carry):
            t = p * half + k
            total = add_up(
                [scores[t, r * SUB:(r + 1) * SUB, :] * spread[r * SUB:(r + 1) * SUB, :]
                 for r in range(rows // SUB)]
            )
            total = jnp.sum(total, axis=0, keepdims=True) * base[pl.ds(t, 1), :]
            col_first[step, p, me, pl.ds(k, 1), :] = total
            return carry

        return body

    for step in range(ITERS):
        send_rows(step)
        if step == 0:
            potential = -log_rows - lse_of(rows_here(step))
            first_rows[...] = potential
            spread_rows(potential)
        else:
            scale = 1.0 / (add_up(rows_here(step)) * (2.0 ** log_rows))
            spread_rows(scale)
        for p in range(2):
            body = col_body(step, p) if step else first_col_body(p)
            lax.fori_loop(0, half, body, 0, unroll=8 if step else 4)
        send_cols(step)
        if step == 0:
            for h in range(row_tiles):
                sq_rows[h:h + 1, :] = squares(src_ref, h)
        if step == ITERS - 1:
            final = first_rows[...] + (jnp.log2(scale) if step else 0.0) + sq_rows[...]
            rows_ref[...] = final * (1.0 / SCALE)
        combine = add_up if step else lse_of
        turn_cols(step, combine)
        for p in range(2):
            at = slice(p * half, (p + 1) * half)
            total = cols_here(step, p, combine)
            if step == 0:
                potential = -log_cols - total
                first_cols[at, :] = potential
                base[at, :] = jnp.exp2(col_peaks[at, :] + potential)
                factors[at, :] = base[at, :]
            else:
                scale = 1.0 / (total * (2.0 ** log_cols))
                factors[at, :] = base[at, :] * scale
                col_scale[at, :] = scale
            if step < ITERS - 1:
                held = [
                    jnp.broadcast_to(factors[p * half + k:p * half + k + 1, :], (SUB, LANES))
                    for k in range(half)
                ]

                def row_body(r, carry, p=p, held=held):
                    at = pl.ds(pl.multiple_of(r * SUB, SUB), SUB)
                    terms = [scores[p * half + k, at, :] * held[k] for k in range(half)]
                    if p:
                        terms.append(across[at, :])
                    across[at, :] = add_up(terms)
                    return carry

                lax.fori_loop(0, rows // SUB, row_body, 0, unroll=8)
        if step < ITERS - 1:
            for h in range(row_tiles):
                total = jnp.sum(across[h * LANES:(h + 1) * LANES, :].T, axis=0, keepdims=True)
                row_slots[step + 1, me_t, h:h + 1, :] = total

    tall = 2 * SUB

    def weight_body(b, carry):
        place = lax.div(b * tall, share)
        within = lax.rem(b * tall, share)
        which = lax.rem(other + lax.div(place, xs), cores)
        start = (lax.rem(place, xs) * cores + which) * share + within
        at = pl.ds(pl.multiple_of(start, tall), tall)
        to = pl.ds(pl.multiple_of(b * tall, tall), tall)
        values = [scores[t, at, :] * factors[t:t + 1, :] for t in range(col_tiles)]
        for t in range(col_tiles):
            weights[to, t * LANES:(t + 1) * LANES] = values[t].astype(jnp.bfloat16)
        across[at, :] = add_up(values)
        return carry

    lax.fori_loop(0, rows // tall, weight_body, 0, unroll=4)
    chunks = width // CHUNK
    sibling = tgt_id(0, other)

    def core_copy(n):
        return copy_of(
            numer.at[n, pl.ds(0, mine)], core_slots.at[n], core_send.at[n], core_recv.at[n], sibling
        )

    for n in range(chunks):
        numer[n] = jnp.dot(
            weights[...], tgt_ref[:, n * CHUNK:(n + 1) * CHUNK], preferred_element_type=jnp.float32
        )
        core_copy(n).start()
    def x_part(n, dx):
        place = lax.rem(x + dx, xs) * share
        return (
            pl.ds(pl.multiple_of(mine + place, share), share),
            pl.ds(pl.multiple_of(place, share), share),
        )

    for n in range(chunks):
        core_copy(n).wait_recv()
        for k, dx in enumerate(x_order):
            own, got = x_part(n, dx)
            numer[n, own, :] = numer[n, own, :] + core_slots[n, got, :]
            copy_of(
                numer.at[n, own], x_slots.at[n, k], x_send.at[n], x_recv.at[n], tgt_id(dx, core)
            ).start()
        if n == 0:
            for h in range(row_tiles):
                total = jnp.sum(across[h * LANES:(h + 1) * LANES, :].T, axis=0, keepdims=True)
                row_slots[ITERS, me_t, h:h + 1, :] = total
            send_rows(ITERS)

    final = first_cols[...] + jnp.log2(col_scale[...]) + sq_cols[...]
    cols_ref[...] = final * (1.0 / SCALE)
    spread_rows(1.0 / add_up(rows_here(ITERS)))
    scale = spread[pl.ds(pl.multiple_of(me_t * share, share), share), :]

    def x_wait(n):
        return copy_of(x_slots.at[n], x_slots.at[n], x_send.at[n], x_recv.at[n], sibling)

    for n in range(chunks):
        own, got = x_part(n, 0)
        near = numer[n, own, :] + core_slots[n, got, :]
        x_wait(n).wait_recv()
        total = near + add_up([x_slots[n, k] for k in range(xs - 1)])
        for k in range(CHUNK // LANES):
            piece = total[:, k * LANES:(k + 1) * LANES] * scale
            start = n * CHUNK + k * LANES
            bary_ref[:, start:start + LANES] = piece.astype(jnp.bfloat16)

    for step in range(ITERS + 1):
        sent(row_slots.at[step], tgt_ids, row_send.at[step], row_recv.at[step])
    for step in range(ITERS):
        for p in range(2):
            for leg, slots, plan in ((0, col_first, first_leg), (1, col_second, second_leg)):
                sent(
                    slots.at[step, p], plan[p][1], col_send.at[step, leg, p], col_recv.at[step, leg, p]
                )
    for n in range(chunks):
        core_copy(n).wait_send()
        x_wait(n).wait_send()


def emit(bary, rows, cols, bary_out, rows_out, cols_out, sems):
    copies = [
        pltpu.make_async_copy(held, out, sems.at[k])
        for k, (held, out) in enumerate(((bary, bary_out), (rows, rows_out), (cols, cols_out)))
    ]
    for copy in copies:
        copy.start()
    for copy in copies:
        copy.wait()


def build(mesh, dims):
    ys, zs, xs, cores = dims
    tgts = xs * cores
    most = max(ys, zs)

    def on_device(sources, targets):
        rows, width = sources.shape
        cols = targets.shape[0]
        row_tiles, col_tiles = rows // LANES, cols // LANES
        half, share, chunks = col_tiles // 2, rows // tgts, width // CHUNK
        f32 = jnp.float32
        dma = pltpu.SemaphoreType.DMA
        bary, dual_rows, dual_cols = pl.pallas_call(
            functools.partial(kernel, dims),
            out_shape=(
                jax.ShapeDtypeStruct((share, width), jnp.bfloat16),
                jax.ShapeDtypeStruct((row_tiles, LANES), f32),
                jax.ShapeDtypeStruct((col_tiles, LANES), f32),
            ),
            in_specs=[pl.BlockSpec(memory_space=pl.ANY)] * 2,
            out_specs=[pl.BlockSpec(memory_space=pltpu.VMEM)] * 3,
            scratch_shapes=[
                pltpu.VMEM((rows, width), jnp.bfloat16),
                pltpu.VMEM((cols, width), jnp.bfloat16),
                pltpu.VMEM((col_tiles, rows, LANES), f32),
                pltpu.VMEM((row_tiles, LANES), f32),
                pltpu.VMEM((col_tiles, LANES), f32),
                pltpu.VMEM((row_tiles, LANES), f32),
                pltpu.VMEM((col_tiles, LANES), f32),
                pltpu.VMEM((col_tiles, LANES), f32),
                pltpu.VMEM((col_tiles, LANES), f32),
                pltpu.VMEM((col_tiles, LANES), f32),
                pltpu.VMEM((col_tiles, LANES), f32),
                pltpu.VMEM((rows, LANES), f32),
                pltpu.VMEM((rows, LANES), f32),
                pltpu.VMEM((rows, cols), jnp.bfloat16),
                pltpu.VMEM((chunks, rows, CHUNK), f32),
                pltpu.VMEM((ITERS + 1, tgts, row_tiles, LANES), f32),
                pltpu.VMEM((ITERS, 2, most, half, LANES), f32),
                pltpu.VMEM((ITERS, 2, most, half, LANES), f32),
                pltpu.VMEM((chunks, rows // cores, CHUNK), f32),
                pltpu.VMEM((chunks, xs - 1, share, CHUNK), f32),
                dma,
                dma((cols // LOAD,)),
                dma((ITERS + 1,)),
                dma((ITERS + 1,)),
                dma((ITERS, 2, 2)),
                dma((ITERS, 2, 2)),
                dma((chunks,)),
                dma((chunks,)),
                dma((chunks,)),
                dma((chunks,)),
            ],
            compiler_params=pltpu.CompilerParams(
                collective_id=0, has_side_effects=True, vmem_limit_bytes=VMEM_GRANT
            ),
        )(sources, targets)
        bary, dual_rows, dual_cols = pl.pallas_call(
            emit,
            out_shape=(
                jax.ShapeDtypeStruct(bary.shape, bary.dtype),
                jax.ShapeDtypeStruct(dual_rows.shape, f32),
                jax.ShapeDtypeStruct(dual_cols.shape, f32),
            ),
            in_specs=[pl.BlockSpec(memory_space=pl.ANY)] * 3,
            out_specs=[pl.BlockSpec(memory_space=pl.ANY)] * 3,
            scratch_shapes=[dma((3,))],
            compiler_params=pltpu.CompilerParams(vmem_limit_bytes=1024 * 1024),
        )(bary, dual_rows, dual_cols)
        return bary, dual_rows.reshape(rows), dual_cols.reshape(cols)

    in_specs = (P("src", None), P("tgt", None))
    out_specs = (P(("src", "tgt"), None), P("src"), P("tgt"))
    return jax.shard_map(
        on_device, mesh=mesh, in_specs=in_specs, out_specs=out_specs, check_vma=False
    )


def solution(mesh):
    return build(mesh, (8, 8, 4, 2))
```
